512 devices in a mesh: row: 16 (over z), col: 32 (over y, x, core).
Axes of the slice: x: 4, y: 4, z: 16, core: 2. Of those that a mesh axis runs over, the one named last changes fastest.
Arguments:
- view_images: float32 [8, 3, 2048, 4096], P(None, None, 'row', 'col'), may hold values from -4 to 4
- intersection_bits: int32 [16, 32], P('row', 'col'), may hold values from 1 to 255
- seam_labels: int32 [16, 32], P('row', 'col'), may hold values from 0 to 7
Outputs:
- panorama: float32 [3, 2048, 4096], P(None, 'row', 'col')
The draws below stay inside these ranges and needn't reach their ends.
All inputs are finite; a program needn't handle non-finite values.
Results may differ from the reference program's by a relative error of at most 0.0001.
Values sent between devices are 32-bit elements; how exact they have to be, the bound alone decides.
A program may use at most 128 MiB of HBM per device.

```python
import jax
import jax.numpy as jnp
from jax import lax

V = 8
C = 3
LEVELS = 8
BLOCK = 128
NH = 2048
NW = 4096
NBR = 16
NBC = 32


def draw_view_images(key, part):
    key = jax.random.fold_in(key, 11)
    key_jitter, key_offset, key_slope = jax.random.split(key, 3)
    offset = jax.random.uniform(key_offset, (V, C, 1, 1), jnp.float32, -0.5, 0.5)
    slopes = jax.random.uniform(key_slope, (2, V, 1, 1, 1), jnp.float32, -1.0, 1.0)
    row_ramp = (2.0 * (jnp.arange(NH, dtype=jnp.float32) + 0.5) / NH - 1.0)[None, None, :, None]
    col_ramp = (2.0 * (jnp.arange(NW, dtype=jnp.float32) + 0.5) / NW - 1.0)[None, None, None, :]
    ramps = slopes[0] * row_ramp + slopes[1] * col_ramp
    jitter = jnp.clip(0.5 * jax.random.normal(key_jitter, (V, C, NH, NW), jnp.float32), -1.5, 1.5)
    return jitter + offset + ramps


def plant(array, own_key, low, high):
    extent = array.shape
    place = [jax.random.randint(jax.random.fold_in(own_key, axis), (), 0, extent[axis]) for axis in range(len(extent))]
    array = array.at[tuple(place)].set(low)
    longest = extent.index(max(extent))
    place[longest] = (place[longest] + 1) % extent[longest]
    return array.at[tuple(place)].set(high)


def setup_inputs(seed: int = 0) -> dict:
    arg_keys = jax.random.split(jax.random.key(seed), 4)
    view_images = draw_view_images(jax.random.fold_in(arg_keys[3], 71), 0)
    intersection_bits = plant(jax.random.randint(arg_keys[1], (NBR, NBC), 1, 256), jax.random.fold_in(arg_keys[1], 1), 1, 255).astype(jnp.int32)
    seam_labels = plant(jax.random.randint(arg_keys[2], (NBR, NBC), 0, 8), jax.random.fold_in(arg_keys[2], 1), 0, 7).astype(jnp.int32)
    return {"view_images": view_images, "intersection_bits": intersection_bits, "seam_labels": seam_labels}


BINOMIAL = (1.0, 4.0, 6.0, 4.0, 1.0)


def border(field, rim_width):
    return jnp.pad(field, ((0, 0), (rim_width, rim_width), (rim_width, rim_width)))


def shrink_axis(padded_in, rim_width, margin, along_axis):
    out_len = (padded_in.shape[along_axis] - 2 * rim_width) // 2 + 2 * margin
    accumulated = None
    for tap_index in range(5):
        begin = rim_width - 2 * margin + tap_index - 2
        sliced = lax.slice_in_dim(padded_in, begin, begin + 2 * out_len - 1, 2, along_axis)
        weighted = BINOMIAL[tap_index] * sliced
        accumulated = weighted if accumulated is None else accumulated + weighted
    return accumulated / 16.0


def spread_axis(coarse_pad, along_axis):
    out_len = coarse_pad.shape[along_axis] - 2
    below_cells = lax.slice_in_dim(coarse_pad, 0, out_len, 1, along_axis)
    centre_cells = lax.slice_in_dim(coarse_pad, 1, out_len + 1, 1, along_axis)
    above_cells = lax.slice_in_dim(coarse_pad, 2, out_len + 2, 1, along_axis)
    even_part = (below_cells + 6.0 * centre_cells + above_cells) / 8.0
    odd_part = (centre_cells + above_cells) / 2.0
    paired = jnp.stack([even_part, odd_part], axis=along_axis + 1)
    out_shape = list(even_part.shape)
    out_shape[along_axis] = 2 * out_len
    return paired.reshape(out_shape)


def reduce_both(padded_in, rim_width, margin):
    return shrink_axis(shrink_axis(padded_in, rim_width, margin, 1), rim_width, margin, 2)


def expand_both(coarse_pad):
    return spread_axis(spread_axis(coarse_pad, 1), 2)


def masks_from(intersection_bits, seam_labels):
    view_ids = jnp.arange(V, dtype=jnp.int32)[:, None, None]
    view_bits = jnp.bitwise_and(jnp.right_shift(intersection_bits[None], view_ids), 1).astype(jnp.float32)
    chosen = (seam_labels[None] == view_ids).astype(jnp.float32)
    block_masks = view_bits * (1.0 + 3.0 * chosen)
    return jnp.repeat(jnp.repeat(block_masks, BLOCK, axis=1), BLOCK, axis=2)


def blend_level(detail, view_masks):
    weight_sum = jnp.sum(view_masks, axis=0)
    shares = view_masks / weight_sum
    layered = detail.reshape(V, C, detail.shape[1], detail.shape[2])
    return jnp.sum(shares[:, None] * layered, axis=0)


def compensate(top_images):
    layered = top_images.reshape(V, C, top_images.shape[1], top_images.shape[2])
    view_means = jnp.mean(layered, axis=(2, 3), keepdims=True)
    common_mean = jnp.mean(view_means, axis=0, keepdims=True)
    return (layered - view_means + common_mean).reshape(top_images.shape)


def collapse(images, view_masks, steps_down):
    blended = []
    for level_index in range(steps_down):
        coarser = reduce_both(border(images, 2), 2, 0)
        coarse_masks = reduce_both(border(view_masks, 2), 2, 0)
        detail = images - expand_both(border(coarser, 1))
        blended.append(blend_level(detail, view_masks))
        images, view_masks = coarser, coarse_masks
    result = blend_level(compensate(images), view_masks)
    for level_index in reversed(range(steps_down)):
        result = blended[level_index] + expand_both(border(result, 1))
    return result


def reference(view_images, intersection_bits, seam_labels):
    images = view_images.reshape(V * C, NH, NW)
    return collapse(images, masks_from(intersection_bits, seam_labels), LEVELS - 1)
```

```python
import numpy as np
import jax
import jax.numpy as jnp
import ml_dtypes
from jax import lax
from jax.experimental import pallas as pl
from jax.experimental.pallas import tpu as pltpu
from jax.sharding import PartitionSpec as P

V = 8
C = 3
BLOCK = 128
LANES = 128
F32 = jnp.float32
MESH = pl.DeviceIdType.MESH

SIDE = [BLOCK >> level for level in range(8)]
ROW0 = {1: 0, 2: 80, 3: 128, 4: 160}
ROWS = {1: 80, 2: 48, 3: 32, 4: 24}
LANE0 = {1: 0, 2: 80, 3: 0, 4: 32}
HALF = {1: 0, 2: 0, 3: 1, 4: 1}
ROW5, LANE5 = 184, 64
FLAT0 = {5: 0, 6: 49, 7: 74}
FLATW = {5: 7, 6: 5, 7: 4}
COPY0 = 73


def shrink_matrix(n):
    m = np.zeros((n // 2, n))
    for k in range(n // 2):
        for a, w in zip(range(-2, 3), (1.0, 4.0, 6.0, 4.0, 1.0)):
            if 0 <= 2 * k + a < n:
                m[k, 2 * k + a] += w / 16.0
    return m


def spread_matrix(n):
    m = np.zeros((2 * n, n))
    for k in range(n):
        for j, w in ((k - 1, 1 / 8), (k, 6 / 8), (k + 1, 1 / 8)):
            if 0 <= j < n:
                m[2 * k, j] += w
        for j in (k, k + 1):
            if j < n:
                m[2 * k + 1, j] += 0.5
    return m


def tile_constants():
    tiles = 10
    total = tiles * BLOCK
    down = [np.eye(total)]
    for level in range(7):
        down.append(shrink_matrix(total >> level) @ down[-1])
    step = [spread_matrix(total >> (level + 1)) for level in range(7)]
    up = [None, step[0]]
    for level in range(1, 7):
        up.append(up[-1] @ step[level])

    def rows_of(matrix, level, t, low, high):
        n = SIDE[level]
        out = np.zeros((high - low + 1, matrix.shape[1]))
        for i, k in enumerate(range(n * t + low, n * t + high + 1)):
            if 0 <= k < matrix.shape[0]:
                out[i] = matrix[k]
        return out

    mats, cols, rows = [], [], []
    for t in (0, 1, 5, 8, 9):
        here = slice(BLOCK * t, BLOCK * (t + 1))
        wide = {l: rows_of(down[l], l, t, -4, SIDE[l] + 4) for l in range(1, 5)}
        parts = []
        for l in range(1, 5):
            span = slice(LANE0[l], LANE0[l] + SIDE[l] + 9)
            own, finer = np.zeros((BLOCK, LANES)), np.zeros((BLOCK, LANES))
            own[:, span] = wide[l][:, here].T
            finer[:, span] = -rows_of(step[l] @ down[l + 1], l, t, -4, SIDE[l] + 4)[:, here].T
            parts += [own, finer]
        copies = np.zeros((BLOCK, LANES))
        one = wide[1][:, here].T
        copies[:, 3:69] = one[:, 3:69]
        copies[:, COPY0 : COPY0 + 2] = one[:, 3:5]
        copies[:, COPY0 + 2 : COPY0 + 4] = one[:, 67:69]
        parts.append(copies)
        column_sum, row_sum = np.zeros((1, LANES)), np.zeros((1, LANES))
        for l in (5, 6, 7):
            w, f = FLATW[l], FLAT0[l]
            local = rows_of(down[l], l, t, -1, w - 2)[:, here]
            flat = np.zeros((BLOCK, LANES))
            flat[:, f : f + w] = local.T
            parts.append(flat)
            total_of = local.sum(axis=1)
            column_sum[0, f : f + w * w] = np.tile(total_of, w)
            row_sum[0, f : f + w * w] = np.repeat(total_of, w)
        mats.append(np.concatenate(parts))

        expand_a, expand_b = np.zeros((LANES, BLOCK)), np.zeros((LANES, BLOCK))
        row_a, row_b = np.zeros((BLOCK, LANES)), np.zeros((BLOCK, LANES))
        for l in range(1, 6):
            n = SIDE[l]
            for k in range(-1, n + 2):
                g = n * t + k
                if not 0 <= g < up[l].shape[1]:
                    continue
                weights = up[l][here, g]
                lane = LANE0[l] + k + 4 if l < 5 else LANE5 + k + 1
                row = ROW0[l] + k + 4 if l < 5 else ROW5 + k + 1
                if l < 3:
                    expand_a[lane] = weights
                    row_a[:, row] = weights
                else:
                    expand_b[lane] = weights
                    row_b[:, row - 128] = weights
        spread_rows, spread_lanes = np.zeros((3, 184, LANES)), np.zeros((8, LANES))
        for d in range(3):
            block = slice(BLOCK * (t + d - 1), BLOCK * (t + d))
            if not 0 <= t + d - 1 < tiles:
                continue
            for l in range(1, 5):
                share = wide[l][:, block].sum(axis=1)
                spread_rows[d, ROW0[l] : ROW0[l] + SIDE[l] + 9] = share[:, None]
                spread_lanes[2 * d + HALF[l], LANE0[l] : LANE0[l] + SIDE[l] + 9] = share
        spread_lanes[6] = column_sum
        weight_of = down[7][:, here].sum(axis=0)
        spread_lanes[7] = weight_of
        cols.append(np.concatenate([expand_a, expand_b, spread_lanes]))
        rows.append(
            np.concatenate(
                [row_a, row_b, spread_rows.reshape(-1, LANES), np.repeat(weight_of[:, None], LANES, 1), np.repeat(row_sum, 8, 0)]
            )
        )
    mats = np.stack(mats).astype(np.float32)
    high = mats.astype(ml_dtypes.bfloat16)
    low = (mats - high.astype(np.float32)).astype(ml_dtypes.bfloat16)
    split = np.stack([high, low], axis=1)

    flat = np.zeros((2, LANES, LANES))
    for which, l in ((0, 7), (1, 6)):
        w, v = FLATW[l], FLATW[l - 1]
        local = np.zeros((v, w))
        for i in range(v):
            m, odd = divmod(i - 1, 2)
            for j, weight in ((m, 0.5), (m + 1, 0.5)) if odd else ((m - 1, 1 / 8), (m, 6 / 8), (m + 1, 1 / 8)):
                local[i, j + 1] += weight
        kron = np.einsum("ai,bj->ijab", local, local).reshape(w * w, v * v)
        flat[which, FLAT0[l] : FLAT0[l] + w * w, FLAT0[l - 1] : FLAT0[l - 1] + v * v] = kron
    return split, np.stack(cols).astype(np.float32), np.stack(rows).astype(np.float32), flat.astype(np.float32)


MATS, COLS, ROWC, FLAT = tile_constants()
N_MATS, N_COLS, N_ROWC = MATS.shape[2], COLS.shape[1], ROWC.shape[1]
COPY_AT = 1024
FLAT_AT = {5: 1152, 6: 1280, 7: 1408}
SPREAD_AT, WEIGHT_AT, RSUM_AT = 256, 808, 936

BEYOND = (1, -1, 2, -2, 3, -3)
AROUND = [(a, b) for a in (-1, 0, 1) for b in (-1, 0, 1) if a or b]
ITEMS = [(c, l, ROW0[l] + 8 * i) for c in range(C) for l in range(1, 5) for i in range(ROWS[l] // 8)]
ITEMS = [item for item in ITEMS if item[2] - ROW0[item[1]] < SIDE[item[1]] + 9]
SIDE_TILES = -(-len(ITEMS) // 16)


def split_dot(a, mat_ref, at, depth, exact=False):
    high = a.astype(jnp.bfloat16)
    low = (a - high.astype(F32)).astype(jnp.bfloat16)
    m_high = mat_ref[0, at : at + depth, :]
    out = jnp.dot(high, m_high, preferred_element_type=F32) + jnp.dot(low, m_high, preferred_element_type=F32)
    if not exact:
        out = out + jnp.dot(high, mat_ref[1, at : at + depth, :], preferred_element_type=F32)
    return out


def lanes_in(low, high, shape=(1, LANES)):
    lane = lax.broadcasted_iota(jnp.int32, shape, len(shape) - 1)
    return jnp.logical_and(lane >= low, lane < high)


def keep(value, low, high):
    return jnp.where(lanes_in(low, high), value, 0.0)


def turn(value, shift):
    shift = shift % LANES
    return pltpu.roll(value, shift, value.ndim - 1) if shift else value


def make_kernel(nr, nc):
    cells = float(nr * nc)

    def kernel(bits_ref, label_ref, x_hbm, mats_hbm, cols_hbm, rows_hbm, flat_hbm, out_ref, *scratch):
        (x_ref, mats, cols, rowc, flat, s1, s2, s3, s4, s5, s6, s7, e1, e2, e3, e4, d1, d2, d3, d4, copies_ref, xs_ref,
         planes, ones_ref, m_send, m_col, m_row, mask_send, mask_recv, t_send, t_row, t_col, v_send, v_recv, h_send,
         h_recv, w_ref, load_sem, send_sem, recv_sem) = scratch
        s = {1: s1, 2: s2, 3: s3, 4: s4, 5: s5, 6: s6, 7: s7}
        e = {1: e1, 2: e2, 3: e3, 4: e4}
        d = {1: d1, 2: d2, 3: d3, 4: d4}
        r = lax.axis_index("row")
        c_at = lax.axis_index("col")

        def place(t, n):
            return jnp.where(t == 0, 0, jnp.where(t == 1, 1, jnp.where(t == n - 1, 4, jnp.where(t == n - 2, 3, 2))))

        def device(dr, dc):
            return (lax.rem(r + dr + nr, nr), lax.rem(c_at + dc + nc, nc))

        def inside(dr, dc):
            rr, cc = r + dr, c_at + dc
            ok = jnp.logical_and(jnp.logical_and(rr >= 0, rr < nr), jnp.logical_and(cc >= 0, cc < nc))
            return ok.astype(jnp.int32).astype(F32)

        row_place, col_place = place(r, nr), place(c_at, nc)
        loads = [
            pltpu.make_async_copy(x_hbm, x_ref, load_sem.at[0]),
            pltpu.make_async_copy(rows_hbm.at[row_place], rowc, load_sem.at[1]),
            pltpu.make_async_copy(cols_hbm.at[col_place], cols, load_sem.at[2]),
            pltpu.make_async_copy(mats_hbm.at[col_place], mats, load_sem.at[3]),
            pltpu.make_async_copy(flat_hbm, flat, load_sem.at[4]),
        ]
        for load in loads:
            load.start()

        barrier = pltpu.get_barrier_semaphore()
        partners = [(0, i) for i in range(1, nc)] + [(i, 0) for i in range(1, nr)]
        partners += [(a, b) for a, b in AROUND if a and b]
        for a, b in partners:
            pl.semaphore_signal(barrier, inc=1, device_id=device(a, b), device_id_type=MESH)

        used = [0]
        sent = []

        def post(src, dst, to):
            slot = used[0]
            used[0] += 1
            copy = pltpu.make_async_remote_copy(
                src_ref=src, dst_ref=dst, send_sem=send_sem.at[slot], recv_sem=recv_sem.at[slot],
                device_id=device(*to), device_id_type=MESH,
            )
            copy.start()
            sent.append(copy)
            return copy

        view = lax.broadcasted_iota(jnp.int32, (V, LANES), 0)
        lane = lax.broadcasted_iota(jnp.int32, (V, LANES), 1)
        bits = jnp.full((V, LANES), bits_ref[0, 0], jnp.int32)
        label = jnp.full((V, LANES), label_ref[0, 0], jnp.int32)
        own_mask = jnp.bitwise_and(jnp.right_shift(bits, view), 1).astype(F32)
        own_mask = own_mask * jnp.where(label == view, 4.0, 1.0)
        mask_send[...] = own_mask

        for l in range(1, 8):
            n = SIDE[l]
            s[l][0:3] = jnp.zeros((3, 24, LANES), F32)
            s[l][n + 6 :] = jnp.zeros((s[l].shape[0] - n - 6, 24, LANES), F32)
        for l in range(1, 5):
            e[l][SIDE[l] + 9 :] = jnp.zeros((ROWS[l] - SIDE[l] - 9, 24, LANES), F32)
        w_ref[...] = jnp.zeros_like(w_ref)

        loads[0].wait()
        loads[1].wait()
        loads[2].wait()

        weight_rows = rowc[WEIGHT_AT : WEIGHT_AT + BLOCK, :]
        weight_cols = cols[256 + 7 : 256 + 8, :]
        mean = jnp.zeros((1, LANES), F32)
        for c in range(C):
            parts = []
            for v in range(V):
                weighted = x_ref[(v * C + c) * BLOCK : (v * C + c + 1) * BLOCK, :] * weight_rows
                parts.append(jnp.sum(weighted.reshape(16, 8, LANES), axis=0)[None])
            both = jnp.sum(jnp.concatenate(parts, axis=0), axis=1) * weight_cols
            total = jnp.sum(both, axis=1, keepdims=True)
            mean = mean + jnp.sum(jnp.where(lane == view + V * c, total, 0.0), axis=0, keepdims=True)
        m_send[0] = mean * (1.0 / cells)

        pl.semaphore_wait(barrier, len(partners))
        m_cols = [post(m_send.at[0], m_col.at[i - 1], (0, i)) for i in range(1, nc)]
        masks = [post(mask_send, mask_recv.at[i], to) for i, to in enumerate(AROUND)]

        def pixel_row(row):
            return jnp.concatenate(
                [x_ref[pl.ds(c * BLOCK + row, V, stride=C * BLOCK), :] for c in range(C)], axis=0
            )

        def tap(get, k):
            total = None
            for a, w in zip(range(-2, 3), (1.0, 4.0, 6.0, 4.0, 1.0)):
                term = get(2 * k + a)
                if term is not None:
                    term = term * (w / 16.0)
                    total = term if total is None else total + term
            return total

        def edge_row(row):
            return pixel_row(row) if 0 <= row < BLOCK else None

        for k in (-1, 0, 63, 64):
            s1[k + 4] = tap(edge_row, k)

        def first_pair(i, carry):
            rows = [pixel_row(4 * i + j) for j in range(7)]
            for half in range(2):
                total = None
                for j, w in enumerate((1.0, 4.0, 6.0, 4.0, 1.0)):
                    term = rows[2 * half + j] * (w / 16.0)
                    total = term if total is None else total + term
                s1[2 * i + half + 5] = total
            return carry

        lax.fori_loop(0, 31, first_pair, 0)
        s1[69] = jnp.zeros((24, LANES), F32)
        not_first = jnp.where(r > 0, 1.0, 0.0)
        not_last = jnp.where(r < nr - 1, 1.0, 0.0)
        not_near = jnp.where(r < nr - 2, 1.0, 0.0)

        def trim(l):
            n = SIDE[l]
            s[l][3] = s[l][3] * not_first
            s[l][n + 4] = s[l][n + 4] * not_last
            s[l][n + 5] = s[l][n + 5] * (not_last if l < 7 else not_near)

        trim(1)
        for l in range(2, 8):
            n = SIDE[l]
            src, dst = s[l - 1], s[l]

            def one(i, src=src, dst=dst):
                total = None
                for j, w in enumerate((1.0, 4.0, 6.0, 4.0, 1.0)):
                    term = src[2 * i + j] * (w / 16.0)
                    total = term if total is None else total + term
                dst[i + 3] = total

            if l == 2:
                def five(i, carry, one=one):
                    for j in range(5):
                        one(5 * i + j)
                    return carry

                lax.fori_loop(0, 7, five, 0)
            else:
                for i in range(n + 3):
                    one(i)
            trim(l)

        loads[3].wait()
        loads[4].wait()
        tops = jnp.zeros((24, LANES), F32)
        for l in (5, 6, 7):
            w = FLATW[l]
            flat_l = split_dot(s[l][3 : 3 + w].reshape(w * 24, LANES), mats, FLAT_AT[l], BLOCK).reshape(w, 24, LANES)
            for i in range(w):
                tops = tops + turn(flat_l[i], i * w)
        t_send[0, 0:24] = tops
        t_send[0, 24:32] = own_mask * (rowc[RSUM_AT : RSUM_AT + 1, :] * cols[256 + 6 : 256 + 7, :])
        t_rows = [post(t_send.at[0], t_row.at[i], (off, 0)) for i, off in enumerate(BEYOND)]

        for l in range(1, 5):
            n, src, dst = SIDE[l], s[l + 1], e[l]

            def pair(i, src=src, dst=dst):
                x0, x1, x2 = src[i + 1], src[i + 2], src[i + 3]
                dst[2 * i] = (x0 + x2) * 0.125 + x1 * 0.75
                return (x1 + x2) * 0.5

            half = n // 2 + 4
            if l < 3:
                def pairs(i, carry, pair=pair, dst=dst):
                    for j in range(4):
                        dst[2 * (4 * i + j) + 1] = pair(4 * i + j)
                    return carry

                lax.fori_loop(0, half // 4, pairs, 0)
            else:
                for i in range(half):
                    dst[2 * i + 1] = pair(i)
            dst[n + 8] = (src[half + 1] + src[half + 3]) * 0.125 + src[half + 2] * 0.75

        chunk = {1: 16, 2: 16, 3: 16, 4: 24}
        for l in range(1, 5):
            m = chunk[l]

            def details(i, carry, l=l, m=m):
                at = pl.multiple_of(i * m, m)
                both = jnp.concatenate(
                    [s[l][pl.ds(at, m)].reshape(m * 24, LANES), e[l][pl.ds(at, m)].reshape(m * 24, LANES)], axis=1
                )
                d[l][pl.ds(at, m)] = split_dot(both, mats, 256 * (l - 1), 256).reshape(m, 24, LANES)
                if l == 1:
                    only = split_dot(both[:, :LANES], mats, COPY_AT, BLOCK, exact=True)
                    copies_ref[pl.ds(at, m)] = only.reshape(m, 24, LANES)
                return carry

            lax.fori_loop(0, ROWS[l] // m, details, 0)

        for copy in m_cols:
            copy.wait_recv()
        m_send[1] = m_send[0] + jnp.sum(m_col[...], axis=0)
        m_rows = [post(m_send.at[1], m_row.at[i - 1], (i, 0)) for i in range(1, nr)]

        def weights(mask):
            total = jnp.sum(mask, axis=0, keepdims=True)
            return mask / jnp.where(total > 0.0, total, 1.0)

        own_weights = weights(own_mask)
        for c in range(C):
            total = None
            for v in range(V):
                term = x_ref[(v * C + c) * BLOCK : (v * C + c + 1) * BLOCK, :] * own_weights[v : v + 1, :]
                total = term if total is None else total + term
            xs_ref[c] = total

        def gather_tops(own, recv, stride, at):
            total = own
            for i, off in enumerate(BEYOND):
                got = recv[i]
                step = -off
                moved = None
                for l in (5, 6, 7):
                    w, n, f = FLATW[l], SIDE[l], FLAT0[l]
                    if w <= n * abs(step):
                        continue
                    index = lax.broadcasted_iota(jnp.int32, (1, LANES), 1) - f
                    along = index // w if stride == "row" else index % w
                    ok = lanes_in(f, f + w * w)
                    ok = jnp.logical_and(ok, jnp.logical_and(along - n * step >= 0, along - n * step < w))
                    term = jnp.where(ok, turn(got, n * step * (w if stride == "row" else 1)), 0.0)
                    moved = term if moved is None else moved + term
                total = total + moved * (inside(step, 0) if stride == "row" else inside(0, step))
            return total

        for copy in t_rows:
            copy.wait_recv()
        t_send[1] = gather_tops(t_send[0], t_row, "row", r)
        t_cols = [post(t_send.at[1], t_col.at[i], (0, off)) for i, off in enumerate(BEYOND)]

        for copy in masks:
            copy.wait_recv()
        around = {(0, 0): own_mask}
        for i, (a, b) in enumerate(AROUND):
            around[(-a, -b)] = mask_recv[i] * inside(-a, -b)
        inner = [
            [
                sum(around[(a, b)] * cols[256 + 2 * (b + 1) + h : 257 + 2 * (b + 1) + h, :] for b in (-1, 0, 1))
                for a in (-1, 0, 1)
            ]
            for h in range(2)
        ]

        def side_weights(a):
            left, mid, right = (weights(around[(a, b)]) for b in (-1, 0, 1))
            value = jnp.where(jnp.logical_and(lane >= COPY0, lane < COPY0 + 2), left, mid)
            return jnp.where(jnp.logical_and(lane >= COPY0 + 2, lane < COPY0 + 4), right, value)

        row_weights = {a: side_weights(a) for a in (-1, 0, 1)}

        for l in range(1, 5):

            def blend(i, carry, l=l):
                at = pl.multiple_of(i * 8, 8)
                row = pl.multiple_of(ROW0[l] + i * 8, 8)
                mask = None
                for a in range(3):
                    term = rowc[pl.ds(SPREAD_AT + 184 * a + row, 8), :][:, None, :] * inner[HALF[l]][a][None]
                    mask = term if mask is None else mask + term
                whole = jnp.sum(mask, axis=1)
                inverse = jnp.where(whole > 0.0, 1.0 / jnp.where(whole > 0.0, whole, 1.0), 0.0)
                for c in range(C):
                    part = d[l][pl.ds(at, 8), V * c : V * c + V, :]
                    planes[c, pl.ds(row, 8), :] = jnp.sum(part * mask, axis=1) * inverse
                    if l == 1:
                        part = copies_ref[pl.ds(at, 8), V * c : V * c + V, :]
                        ones_ref[c, pl.ds(at, 8), :] = jnp.sum(part * row_weights[0][None], axis=1)
                return carry

            lax.fori_loop(0, ROWS[l] // 8, blend, 0)

        for c in range(C):
            v_send[0, c, 0] = planes[c, 0:8] + planes[c, 80:88]
            v_send[0, c, 1] = planes[c, 128:136] + planes[c, 160:168]
            part = copies_ref[0:8, V * c : V * c + V, :]
            v_send[0, c, 2] = jnp.sum(part * row_weights[-1][None], axis=1)
            v_send[1, c, 0] = planes[c, 67:75] + planes[c, 115:123]
            v_send[1, c, 1] = planes[c, 147:155] + planes[c, 171:179]
            part = copies_ref[67:75, V * c : V * c + V, :]
            v_send[1, c, 2] = jnp.sum(part * row_weights[1][None], axis=1)
        v_rows = [post(v_send.at[0], v_recv.at[0], (-1, 0)), post(v_send.at[1], v_recv.at[1], (1, 0))]

        for copy in t_cols:
            copy.wait_recv()
        tops_all = gather_tops(t_send[1], t_col, "col", c_at)
        images, mask = tops_all[0:24], tops_all[24:32]
        whole = jnp.sum(mask, axis=0, keepdims=True)
        here = whole > 0.0
        share = mask * jnp.where(here, 1.0 / jnp.where(here, whole, 1.0), 0.0)
        finer = jnp.dot(images, flat[0] + flat[1], precision=lax.Precision.HIGHEST, preferred_element_type=F32)
        detail = images - finer
        blended = [jnp.sum(detail[V * c : V * c + V] * share, axis=0, keepdims=True) for c in range(C)]
        balance = keep(jnp.sum(share, axis=0, keepdims=True) * (1.0 / V) - share, FLAT0[7], FLAT0[7] + 16)
        chain = jnp.concatenate(blended + [jnp.zeros((8 - C, LANES), F32), balance], axis=0)
        for which in range(2):
            step = jnp.dot(chain, flat[which], precision=lax.Precision.HIGHEST, preferred_element_type=F32)
            chain = chain + jnp.where(here, step, 0.0)
        for c in range(C):
            w_ref[V * c : V * c + V] = chain[8:16]

        for copy in v_rows:
            copy.wait_recv()
        for which, away in ((1, -1), (0, 1)):
            flag = inside(away, 0)
            for c in range(C):
                for l in range(1, 5):
                    at = ROW0[l] + (3 if away < 0 else SIDE[l])
                    low = LANE0[l]
                    got = v_recv[which, c, HALF[l]][0:6] * flag
                    planes[c, at : at + 6] += keep(got, low, low + SIDE[l] + 9)
                at = 3 if away < 0 else SIDE[1]
                ones_ref[c, at : at + 6] += v_recv[which, c, 2][0:6] * flag
        for which in range(2):
            for g in range(SIDE_TILES):
                tile = jnp.zeros((8, LANES), F32)
                for u, (c, l, row) in enumerate(ITEMS[16 * g : 16 * g + 16]):
                    first = LANE0[l] + (SIDE[l] + 3 if which else 0)
                    tile = tile + keep(turn(planes[c, row : row + 8], 8 * u - first), 8 * u, 8 * u + 6)
                    if l == 1:
                        slot, first = (8 * u, COPY0 + 2) if which else (8 * u + 3, COPY0)
                        tile = tile - keep(turn(ones_ref[c, row : row + 8], slot - first), slot, slot + 2)
                h_send[which, g] = tile
        h_cols = [post(h_send.at[0], h_recv.at[0], (0, -1)), post(h_send.at[1], h_recv.at[1], (0, 1))]

        for c in range(C):
            planes[c, 0:80] -= keep(ones_ref[c], 0, COPY0)
            planes[c, ROW5 : ROW5 + 8] = jnp.zeros((8, LANES), F32)

        for copy in m_rows:
            copy.wait_recv()
        means = m_send[1] + jnp.sum(m_row[...], axis=0)
        picked = jnp.where(lane // V == view, jnp.broadcast_to(means, (V, LANES)), 0.0)
        level5 = chain[0:8] + jnp.dot(picked, w_ref[...], precision=lax.Precision.HIGHEST, preferred_element_type=F32)
        for i in range(7):
            line = keep(turn(level5, LANE5 - 7 * i), LANE5, LANE5 + 7)
            for c in range(C):
                planes[c, ROW5 + i : ROW5 + i + 1] = line[c : c + 1]

        for copy in h_cols:
            copy.wait_recv()
        for which, away in ((1, -1), (0, 1)):
            flag = inside(0, away)
            for i, (c, l, row) in enumerate(ITEMS):
                u = i % 16
                first = LANE0[l] + (3 if away < 0 else SIDE[l])
                got = h_recv[which, i // 16] * flag
                planes[c, row : row + 8] += keep(turn(got, first - 8 * u), first, first + 6)

        for c in range(C):
            upper = jnp.dot(rowc[0:128], planes[c, 0:128], precision=lax.Precision.HIGH, preferred_element_type=F32)
            lower = jnp.dot(rowc[128:256, 0:64], planes[c, 128:192], precision=lax.Precision.HIGH, preferred_element_type=F32)
            total = jnp.dot(upper, cols[0:128], precision=lax.Precision.HIGH, preferred_element_type=F32)
            total = total + jnp.dot(lower, cols[128:256], precision=lax.Precision.HIGH, preferred_element_type=F32)
            out_ref[c] = xs_ref[c] + total

        for copy in sent:
            copy.wait_send()

    def vmem(*shape):
        return pltpu.VMEM(shape, F32)

    slabs = [vmem(n, 24, LANES) for n in (80, 48, 32, 24, 16, 16, 16)]
    wides = [vmem(ROWS[l], 24, LANES) for l in range(1, 5)]
    scratch = [
        vmem(V * C * BLOCK, LANES),
        pltpu.VMEM((2, N_MATS, LANES), jnp.bfloat16),
        vmem(N_COLS, LANES),
        vmem(N_ROWC, LANES),
        vmem(2, LANES, LANES),
        *slabs, *wides, *wides,
        vmem(80, 24, LANES),
        vmem(C, BLOCK, LANES),
        vmem(C, 192, LANES),
        vmem(C, 80, LANES),
        vmem(2, 1, LANES),
        vmem(nc - 1, 1, LANES),
        vmem(nr - 1, 1, LANES),
        vmem(V, LANES),
        vmem(8, V, LANES),
        vmem(2, 32, LANES),
        vmem(6, 32, LANES),
        vmem(6, 32, LANES),
        vmem(2, C, 3, 8, LANES),
        vmem(2, C, 3, 8, LANES),
        vmem(2, SIDE_TILES, 8, LANES),
        vmem(2, SIDE_TILES, 8, LANES),
        vmem(LANES, LANES),
        pltpu.SemaphoreType.DMA((5,)),
        pltpu.SemaphoreType.DMA((nr + nc + 22,)),
        pltpu.SemaphoreType.DMA((nr + nc + 22,)),
    ]
    return pl.pallas_call(
        kernel,
        out_shape=jax.ShapeDtypeStruct((C, BLOCK, BLOCK), F32),
        in_specs=[pl.BlockSpec(memory_space=pltpu.SMEM)] * 2 + [pl.BlockSpec(memory_space=pl.ANY)] * 5,
        out_specs=pl.BlockSpec(memory_space=pltpu.VMEM),
        scratch_shapes=scratch,
        compiler_params=pltpu.CompilerParams(collective_id=0, has_side_effects=True, vmem_limit_bytes=48 << 20),
    )


def solution(mesh):
    call = make_kernel(mesh.shape["row"], mesh.shape["col"])

    def local(view_images, intersection_bits, seam_labels):
        planes = view_images.reshape(V * C * BLOCK, BLOCK)
        return call(
            intersection_bits, seam_labels, planes,
            jnp.asarray(MATS), jnp.asarray(COLS), jnp.asarray(ROWC), jnp.asarray(FLAT),
        )

    placed = (P(None, None, "row", "col"), P("row", "col"), P("row", "col"))
    return jax.shard_map(local, mesh=mesh, in_specs=placed, out_specs=P(None, "row", "col"), check_vma=False)
```

```python
import numpy as np
import jax
import jax.numpy as jnp
import ml_dtypes
from jax import lax
from jax.experimental import pallas as pl
from jax.experimental.pallas import tpu as pltpu
from jax.sharding import PartitionSpec as P

V = 8
C = 3
BLOCK = 128
LANES = 128
F32 = jnp.float32
MESH = pl.DeviceIdType.MESH

SIDE = [BLOCK >> level for level in range(8)]
ROW0 = {1: 0, 2: 80, 3: 128, 4: 160}
ROWS = {1: 80, 2: 48, 3: 32, 4: 24}
LANE0 = {1: 0, 2: 80, 3: 0, 4: 32}
HALF = {1: 0, 2: 0, 3: 1, 4: 1}
ROW5, LANE5 = 184, 64
FLAT0 = {5: 0, 6: 49, 7: 74}
FLATW = {5: 7, 6: 5, 7: 4}
COPY0 = 73


def shrink_matrix(n):
    m = np.zeros((n // 2, n))
    for k in range(n // 2):
        for a, w in zip(range(-2, 3), (1.0, 4.0, 6.0, 4.0, 1.0)):
            if 0 <= 2 * k + a < n:
                m[k, 2 * k + a] += w / 16.0
    return m


def spread_matrix(n):
    m = np.zeros((2 * n, n))
    for k in range(n):
        for j, w in ((k - 1, 1 / 8), (k, 6 / 8), (k + 1, 1 / 8)):
            if 0 <= j < n:
                m[2 * k, j] += w
        for j in (k, k + 1):
            if j < n:
                m[2 * k + 1, j] += 0.5
    return m


def tile_constants():
    tiles = 10
    total = tiles * BLOCK
    down = [np.eye(total)]
    for level in range(7):
        down.append(shrink_matrix(total >> level) @ down[-1])
    step = [spread_matrix(total >> (level + 1)) for level in range(7)]
    up = [None, step[0]]
    for level in range(1, 7):
        up.append(up[-1] @ step[level])

    def rows_of(matrix, level, t, low, high):
        n = SIDE[level]
        out = np.zeros((high - low + 1, matrix.shape[1]))
        for i, k in enumerate(range(n * t + low, n * t + high + 1)):
            if 0 <= k < matrix.shape[0]:
                out[i] = matrix[k]
        return out

    mats, cols, rows = [], [], []
    for t in (0, 1, 5, 8, 9):
        here = slice(BLOCK * t, BLOCK * (t + 1))
        wide = {l: rows_of(down[l], l, t, -4, SIDE[l] + 4) for l in range(1, 5)}
        parts = {}
        for l in range(1, 5):
            span = slice(LANE0[l], LANE0[l] + SIDE[l] + 9)
            own, finer = np.zeros((BLOCK, LANES)), np.zeros((BLOCK, LANES))
            own[:, span] = wide[l][:, here].T / 16.0**l
            finer[:, span] = -rows_of(step[l] @ down[l + 1], l, t, -4, SIDE[l] + 4)[:, here].T / (8 * 16.0 ** (l + 1))
            parts[l] = np.concatenate([own, finer])
        copies = np.zeros((BLOCK, LANES))
        one = wide[1][:, here].T / 16.0
        copies[:, 3:69] = one[:, 3:69]
        copies[:, COPY0 : COPY0 + 2] = one[:, 3:5]
        copies[:, COPY0 + 2 : COPY0 + 4] = one[:, 67:69]
        column_sum, row_sum = np.zeros((1, LANES)), np.zeros((1, LANES))
        for l in (5, 6, 7):
            w, f = FLATW[l], FLAT0[l]
            local = rows_of(down[l], l, t, -1, w - 2)[:, here]
            flat = np.zeros((BLOCK, LANES))
            flat[:, f : f + w] = local.T / 16.0**l
            parts[l] = flat
            total_of = local.sum(axis=1)
            column_sum[0, f : f + w * w] = np.tile(total_of, w)
            row_sum[0, f : f + w * w] = np.repeat(total_of, w)
        high = {l: part.astype(ml_dtypes.bfloat16) for l, part in parts.items()}
        low = {l: (part - high[l].astype(np.float64)).astype(ml_dtypes.bfloat16) for l, part in parts.items()}
        copies = np.concatenate([copies, np.zeros_like(copies)]).astype(ml_dtypes.bfloat16)
        blocks = [np.concatenate([high[1], copies], axis=1), np.concatenate([low[1], np.zeros_like(copies)], axis=1)]
        blocks += [np.concatenate([high[l], low[l]], axis=1) for l in range(2, 8)]
        mats.append(np.concatenate(blocks))

        expand_a, expand_b = np.zeros((LANES, BLOCK)), np.zeros((LANES, BLOCK))
        row_a, row_b = np.zeros((BLOCK, LANES)), np.zeros((BLOCK, LANES))
        for l in range(1, 6):
            n = SIDE[l]
            for k in range(-1, n + 2):
                g = n * t + k
                if not 0 <= g < up[l].shape[1]:
                    continue
                weights = up[l][here, g]
                lane = LANE0[l] + k + 4 if l < 5 else LANE5 + k + 1
                row = ROW0[l] + k + 4 if l < 5 else ROW5 + k + 1
                if l < 3:
                    expand_a[lane] = weights
                    row_a[:, row] = weights
                else:
                    expand_b[lane] = weights
                    row_b[:, row - 128] = weights
        spread_rows, spread_lanes = np.zeros((3, 184, LANES)), np.zeros((8, LANES))
        for d in range(3):
            block = slice(BLOCK * (t + d - 1), BLOCK * (t + d))
            if not 0 <= t + d - 1 < tiles:
                continue
            for l in range(1, 5):
                share = wide[l][:, block].sum(axis=1)
                spread_rows[d, ROW0[l] : ROW0[l] + SIDE[l] + 9] = share[:, None]
                spread_lanes[2 * d + HALF[l], LANE0[l] : LANE0[l] + SIDE[l] + 9] = share
        spread_lanes[6] = column_sum
        weight_of = down[7][:, here].sum(axis=0)
        spread_lanes[7] = weight_of
        cols.append(np.concatenate([expand_a, expand_b, spread_lanes]))
        rows.append(
            np.concatenate(
                [row_a, row_b, spread_rows.reshape(-1, LANES), np.repeat(weight_of[:, None], LANES, 1), np.repeat(row_sum, 8, 0)]
            )
        )
    flat = np.zeros((2, LANES, LANES))
    for which, l in ((0, 7), (1, 6)):
        w, v = FLATW[l], FLATW[l - 1]
        local = np.zeros((v, w))
        for i in range(v):
            m, odd = divmod(i - 1, 2)
            for j, weight in ((m, 0.5), (m + 1, 0.5)) if odd else ((m - 1, 1 / 8), (m, 6 / 8), (m + 1, 1 / 8)):
                local[i, j + 1] += weight
        kron = np.einsum("ai,bj->ijab", local, local).reshape(w * w, v * v)
        flat[which, FLAT0[l] : FLAT0[l] + w * w, FLAT0[l - 1] : FLAT0[l - 1] + v * v] = kron
    cols = [np.concatenate([part, flat[0], flat[1]]) for part in cols]
    return np.stack(mats), np.stack(cols).astype(np.float32), np.stack(rows).astype(np.float32)


MATS, COLS, ROWC = tile_constants()
N_MATS, N_COLS, N_ROWC = MATS.shape[1], COLS.shape[1], ROWC.shape[1]
MATS_AT = {1: 0, 2: 512, 3: 768, 4: 1024, 5: 1280, 6: 1408, 7: 1536}
SPREAD_AT, WEIGHT_AT, RSUM_AT, FLAT_AT = 256, 808, 936, 264

BEYOND = (1, -1, 2, -2, 3, -3)
AROUND = [(a, b) for a in (-1, 0, 1) for b in (-1, 0, 1) if a or b]
ITEMS = [(c, l, ROW0[l] + 8 * i) for c in range(C) for l in range(1, 5) for i in range(ROWS[l] // 8)]
ITEMS = [item for item in ITEMS if item[2] - ROW0[item[1]] < SIDE[item[1]] + 9]
SIDE_TILES = -(-len(ITEMS) // 16)


def split(a):
    high = a.astype(jnp.bfloat16)
    return high, (a - high.astype(F32)).astype(jnp.bfloat16)


def split_dot(a, mats, l, depth):
    high, low = split(a)
    at = MATS_AT[l]
    both = jnp.dot(high, mats[at : at + depth, :], preferred_element_type=F32)
    rest = jnp.dot(low, mats[at : at + depth, :LANES], preferred_element_type=F32)
    return both[:, :LANES] + both[:, LANES:] + rest


def lanes_in(low, high, shape=(1, LANES)):
    lane = lax.broadcasted_iota(jnp.int32, shape, len(shape) - 1)
    return jnp.logical_and(lane >= low, lane < high)


def keep(value, low, high):
    return jnp.where(lanes_in(low, high), value, 0.0)


def turn(value, shift):
    shift = shift % LANES
    return pltpu.roll(value, shift, value.ndim - 1) if shift else value


def make_kernel(nr, nc):
    cells = float(nr * nc)

    def kernel(bits_ref, label_ref, x_hbm, mats_hbm, cols_hbm, rows_hbm, out_ref, *scratch):
        (x_ref, mats, cols, rowc, s1, s2, s3, s4, s5, s6, s7, e1, e2, e3, e4, d1, d2, d3, d4, copies_ref, xs_ref,
         planes, ones_ref, m_send, m_col, m_row, mask_send, mask_recv, t_send, t_row, t_col, v_send, v_recv, h_send,
         h_recv, c_send, c_recv, lines_ref, w_ref, load_sem, send_sem, recv_sem, far_sem) = scratch
        s = {1: s1, 2: s2, 3: s3, 4: s4, 5: s5, 6: s6, 7: s7}
        e = {1: e1, 2: e2, 3: e3, 4: e4}
        d = {1: d1, 2: d2, 3: d3, 4: d4}
        r = lax.axis_index("row")
        c_at = lax.axis_index("col")

        def place(t, n):
            return jnp.where(t == 0, 0, jnp.where(t == 1, 1, jnp.where(t == n - 1, 4, jnp.where(t == n - 2, 3, 2))))

        def device(dr, dc):
            return (lax.rem(r + dr + nr, nr), lax.rem(c_at + dc + nc, nc))

        def inside(dr, dc):
            rr, cc = r + dr, c_at + dc
            ok = jnp.logical_and(jnp.logical_and(rr >= 0, rr < nr), jnp.logical_and(cc >= 0, cc < nc))
            return ok.astype(jnp.int32).astype(F32)

        row_place, col_place = place(r, nr), place(c_at, nc)
        part = V * C * BLOCK // 8
        loads = [
            pltpu.make_async_copy(
                rows_hbm.at[row_place, WEIGHT_AT : WEIGHT_AT + BLOCK], rowc.at[WEIGHT_AT : WEIGHT_AT + BLOCK], load_sem.at[0]
            ),
            pltpu.make_async_copy(cols_hbm.at[col_place, :FLAT_AT], cols.at[:FLAT_AT], load_sem.at[1]),
            pltpu.make_async_copy(mats_hbm.at[col_place], mats, load_sem.at[2]),
            pltpu.make_async_copy(rows_hbm.at[row_place, :WEIGHT_AT], rowc.at[:WEIGHT_AT], load_sem.at[3]),
            pltpu.make_async_copy(
                rows_hbm.at[row_place, WEIGHT_AT + BLOCK :], rowc.at[WEIGHT_AT + BLOCK :], load_sem.at[4]
            ),
            pltpu.make_async_copy(cols_hbm.at[col_place, FLAT_AT:], cols.at[FLAT_AT:], load_sem.at[5]),
        ]
        image_loads = [
            pltpu.make_async_copy(
                x_hbm.at[i * part : (i + 1) * part], x_ref.at[i * part : (i + 1) * part], load_sem.at[6 + i // 4]
            )
            for i in range(8)
        ]
        barrier = pltpu.get_barrier_semaphore()
        partners = [(0, i) for i in range(1, nc)] + [(i, 0) for i in (1, -1, 2, -2, 3, -3, 4, -4)]
        partners += [(a, b) for a, b in AROUND if a and b]
        loads[0].start()
        loads[1].start()
        for load in image_loads:
            load.start()
        for load in loads[2:]:
            load.start()
        for a, b in partners:
            pl.semaphore_signal(barrier, inc=1, device_id=device(a, b), device_id_type=MESH)

        groups = []

        def post(whole, copies):
            slot = len(groups)

            def describe(src, dst, to):
                return pltpu.make_async_remote_copy(
                    src_ref=src, dst_ref=dst, send_sem=send_sem.at[slot], recv_sem=recv_sem.at[slot],
                    device_id=device(*to), device_id_type=MESH,
                )

            for src, dst, to in copies:
                describe(src, dst, to).start()
            group = describe(whole, whole, copies[0][2])
            groups.append(group)
            return group

        view = lax.broadcasted_iota(jnp.int32, (V, LANES), 0)
        lane = lax.broadcasted_iota(jnp.int32, (V, LANES), 1)
        bits = jnp.full((V, LANES), bits_ref[0, 0], jnp.int32)
        label = jnp.full((V, LANES), label_ref[0, 0], jnp.int32)
        own_mask = jnp.bitwise_and(jnp.right_shift(bits, view), 1).astype(F32)
        own_mask = own_mask * jnp.where(label == view, 4.0, 1.0)
        mask_send[...] = own_mask

        for l in range(1, 8):
            n = SIDE[l]
            s[l][0:3] = jnp.zeros((3, 24, LANES), F32)
            s[l][n + 6 :] = jnp.zeros((s[l].shape[0] - n - 6, 24, LANES), F32)
        for l in range(1, 5):
            e[l][SIDE[l] + 9 :] = jnp.zeros((ROWS[l] - SIDE[l] - 9, 24, LANES), F32)
        for l, n in ((1, 75), (2, 42), (3, 25), (4, 17)):
            d[l][n:] = jnp.zeros((ROWS[l] - n, 24, LANES), F32)
        copies_ref[75:] = jnp.zeros((5, 24, LANES), F32)
        lines_ref[...] = jnp.zeros_like(lines_ref)

        loads[0].wait()
        loads[1].wait()

        weight_rows = rowc[WEIGHT_AT : WEIGHT_AT + BLOCK, :]
        weight_cols = cols[256 + 7 : 256 + 8, :]
        parts = [[] for _ in range(C)]
        for v in range(V):
            if v % 4 == 0:
                for load in image_loads[v : v + 4]:
                    load.wait()
            for c in range(C):
                weighted = x_ref[(v * C + c) * BLOCK : (v * C + c + 1) * BLOCK, :] * weight_rows
                parts[c].append(jnp.sum(weighted.reshape(16, 8, LANES), axis=0)[None])
        mean = jnp.zeros((1, LANES), F32)
        for c in range(C):
            both = jnp.sum(jnp.concatenate(parts[c], axis=0), axis=1) * weight_cols
            total = jnp.sum(both, axis=1, keepdims=True)
            mean = mean + jnp.sum(jnp.where(lane == view + V * c, total, 0.0), axis=0, keepdims=True)
        m_send[0] = mean * (1.0 / cells)

        def pixel_row(row):
            return jnp.concatenate(
                [x_ref[pl.ds(c * BLOCK + row, V, stride=C * BLOCK), :] for c in range(C)], axis=0
            )

        def tap(get, k):
            total = None
            for a, w in zip(range(-2, 3), (1.0, 4.0, 6.0, 4.0, 1.0)):
                term = get(2 * k + a)
                if term is not None:
                    term = term * w
                    total = term if total is None else total + term
            return total

        def five_taps(x):
            return (x[0] + x[4]) + 4.0 * (x[1] + x[3]) + 6.0 * x[2]

        def edge_row(row):
            return pixel_row(row) if 0 <= row < BLOCK else None

        for k in (-1, 0, 63, 64):
            s1[k + 4] = tap(edge_row, k)

        def first_pair(i, carry):
            rows = [pixel_row(4 * i + j) for j in range(7)]
            for half in range(2):
                s1[2 * i + half + 5] = five_taps(rows[2 * half :])
            return carry

        lax.fori_loop(0, 31, first_pair, 0)
        s1[69] = jnp.zeros((24, LANES), F32)
        not_first = jnp.where(r > 0, 1.0, 0.0)
        not_last = jnp.where(r < nr - 1, 1.0, 0.0)
        not_near = jnp.where(r < nr - 2, 1.0, 0.0)

        def trim(l):
            n = SIDE[l]
            s[l][3] = s[l][3] * not_first
            s[l][n + 4] = s[l][n + 4] * not_last
            s[l][n + 5] = s[l][n + 5] * (not_last if l < 7 else not_near)

        trim(1)
        for l in range(2, 8):
            n = SIDE[l]
            src, dst = s[l - 1], s[l]

            def one(i, src=src, dst=dst):
                dst[i + 3] = five_taps([src[2 * i + j] for j in range(5)])

            if l == 2:
                def five(i, carry, one=one):
                    for j in range(5):
                        one(5 * i + j)
                    return carry

                lax.fori_loop(0, 7, five, 0)
            else:
                for i in range(n + 3):
                    one(i)
            trim(l)

        for load in loads[2:]:
            load.wait()
        tops = jnp.zeros((24, LANES), F32)
        for l in (5, 6, 7):
            w = FLATW[l]
            flat_l = split_dot(s[l][3 : 3 + w].reshape(w * 24, LANES), mats, l, BLOCK).reshape(w, 24, LANES)
            for i in range(w):
                tops = tops + turn(flat_l[i], i * w)
        t_send[0, 0:24] = tops
        t_send[0, 24:32] = own_mask * (rowc[RSUM_AT : RSUM_AT + 1, :] * cols[256 + 6 : 256 + 7, :])

        pl.semaphore_wait(barrier, len(partners))
        for away in (4, -4):
            pl.semaphore_signal(far_sem, inc=1, device_id=device(away, 0), device_id_type=MESH)
        m_cols = post(m_col, [(m_send.at[0], m_col.at[i - 1], (0, i)) for i in range(1, nc)])
        masks = post(mask_recv, [(mask_send, mask_recv.at[i], to) for i, to in enumerate(AROUND)])
        t_rows = post(t_row, [(t_send.at[0], t_row.at[i], (off, 0)) for i, off in enumerate(BEYOND)])

        for l in range(1, 5):
            n, src, dst = SIDE[l], s[l + 1], e[l]

            def pair(i, src=src, dst=dst):
                x0, x1, x2 = src[i + 1], src[i + 2], src[i + 3]
                dst[2 * i] = (x0 + x2) + 6.0 * x1
                return 4.0 * (x1 + x2)

            half = n // 2 + 4
            if l < 3:
                def pairs(i, carry, pair=pair, dst=dst):
                    for j in range(4):
                        dst[2 * (4 * i + j) + 1] = pair(4 * i + j)
                    return carry

                lax.fori_loop(0, half // 4, pairs, 0)
            else:
                for i in range(half):
                    dst[2 * i + 1] = pair(i)
            dst[n + 8] = (src[half + 1] + src[half + 3]) + 6.0 * src[half + 2]

        for l, m, times in ((1, 15, 5), (2, 14, 3), (3, 25, 1), (4, 17, 1)):

            def details(i, carry, l=l, m=m):
                at = i * m
                both = jnp.concatenate(
                    [s[l][pl.ds(at, m)].reshape(m * 24, LANES), e[l][pl.ds(at, m)].reshape(m * 24, LANES)], axis=1
                )
                if l > 1:
                    d[l][pl.ds(at, m)] = split_dot(both, mats, l, 256).reshape(m, 24, LANES)
                else:
                    high, low = split(both)
                    wide = jnp.dot(high, mats[0:256, :], preferred_element_type=F32)
                    wide = wide + jnp.dot(low, mats[0:256, :], preferred_element_type=F32)
                    rest = jnp.dot(high, mats[256:512, :LANES], preferred_element_type=F32)
                    d[l][pl.ds(at, m)] = (wide[:, :LANES] + rest).reshape(m, 24, LANES)
                    copies_ref[pl.ds(at, m)] = wide[:, LANES:].reshape(m, 24, LANES)
                return carry

            if times > 1:
                lax.fori_loop(0, times, details, 0)
            else:
                details(0, 0)

        def weights(mask):
            total = jnp.sum(mask, axis=0, keepdims=True)
            return mask / jnp.where(total > 0.0, total, 1.0)

        own_weights = weights(own_mask)
        for c in range(C):
            total = None
            for v in range(V):
                term = x_ref[(v * C + c) * BLOCK : (v * C + c + 1) * BLOCK, :] * own_weights[v : v + 1, :]
                total = term if total is None else total + term
            xs_ref[c] = total

        def gather_tops(own, recv, stride, at):
            total = own
            for i, off in enumerate(BEYOND):
                got = recv[i]
                step = -off
                moved = None
                for l in (5, 6, 7):
                    w, n, f = FLATW[l], SIDE[l], FLAT0[l]
                    if w <= n * abs(step):
                        continue
                    index = lax.broadcasted_iota(jnp.int32, (1, LANES), 1) - f
                    along = index // w if stride == "row" else index % w
                    ok = lanes_in(f, f + w * w)
                    ok = jnp.logical_and(ok, jnp.logical_and(along - n * step >= 0, along - n * step < w))
                    term = jnp.where(ok, turn(got, n * step * (w if stride == "row" else 1)), 0.0)
                    moved = term if moved is None else moved + term
                total = total + moved * (inside(step, 0) if stride == "row" else inside(0, step))
            return total

        t_rows.wait_recv()
        t_send[1] = gather_tops(t_send[0], t_row, "row", r)
        t_cols = post(t_col, [(t_send.at[1], t_col.at[i], (0, off)) for i, off in enumerate(BEYOND)])

        m_cols.wait_recv()
        pl.semaphore_wait(far_sem, 2)
        m_send[1] = m_send[0] + jnp.sum(m_col[...], axis=0)
        m_rows = post(m_row, [(m_send.at[1], m_row.at[i - 1], (i, 0)) for i in range(1, nr)])

        masks.wait_recv()
        around = {(0, 0): own_mask}
        for i, (a, b) in enumerate(AROUND):
            around[(-a, -b)] = mask_recv[i] * inside(-a, -b)
        inner = [
            [
                sum(around[(a, b)] * cols[256 + 2 * (b + 1) + h : 257 + 2 * (b + 1) + h, :] for b in (-1, 0, 1))
                for a in (-1, 0, 1)
            ]
            for h in range(2)
        ]

        def side_weights(a):
            left, mid, right = (weights(around[(a, b)]) for b in (-1, 0, 1))
            value = jnp.where(jnp.logical_and(lane >= COPY0, lane < COPY0 + 2), left, mid)
            return jnp.where(jnp.logical_and(lane >= COPY0 + 2, lane < COPY0 + 4), right, value)

        row_weights = {a: side_weights(a) for a in (-1, 0, 1)}

        for l in range(1, 5):

            def blend(i, carry, l=l):
                at = pl.multiple_of(i * 8, 8)
                row = pl.multiple_of(ROW0[l] + i * 8, 8)
                mask = None
                for a in range(3):
                    term = rowc[pl.ds(SPREAD_AT + 184 * a + row, 8), :][:, None, :] * inner[HALF[l]][a][None]
                    mask = term if mask is None else mask + term
                whole = jnp.sum(mask, axis=1)
                inverse = jnp.where(whole > 0.0, 1.0 / jnp.where(whole > 0.0, whole, 1.0), 0.0)
                for c in range(C):
                    part = d[l][pl.ds(at, 8), V * c : V * c + V, :]
                    planes[c, pl.ds(row, 8), :] = jnp.sum(part * mask, axis=1) * inverse
                    if l == 1:
                        part = copies_ref[pl.ds(at, 8), V * c : V * c + V, :]
                        ones_ref[c, pl.ds(at, 8), :] = jnp.sum(part * row_weights[0][None], axis=1)
                return carry

            lax.fori_loop(0, ROWS[l] // 8, blend, 0)

        for w in range(2):
            corners = [jnp.zeros((8, LANES), F32) for _ in range(2)]
            for c in range(C):
                at = {l: ROW0[l] + (SIDE[l] + 3 if w else 0) for l in range(1, 5)}
                halves = [planes[c, at[l] : at[l] + 8] + planes[c, at[l + 1] : at[l + 1] + 8] for l in (1, 3)]
                one = copies_ref[at[1] : at[1] + 8, V * c : V * c + V, :]
                one = jnp.sum(one * row_weights[1 if w else -1][None], axis=1)
                v_send[w, c, 0] = halves[0] - keep(one, 0, COPY0)
                v_send[w, c, 1] = halves[1]
                for side in range(2):
                    for l in range(1, 5):
                        slot = 8 * (4 * c + l - 1)
                        first = LANE0[l] + (SIDE[l] + 3 if side else 0)
                        corners[side] += keep(turn(halves[HALF[l]], slot - first), slot, slot + 6)
                    slot, first = (32 * c, COPY0 + 2) if side else (32 * c + 3, COPY0)
                    corners[side] -= keep(turn(one, slot - first), slot, slot + 2)
            for side in range(2):
                c_send[2 * w + side] = corners[side]
        v_rims = post(v_recv, [(v_send.at[w], v_recv.at[w], (2 * w - 1, 0)) for w in range(2)])
        ends = [(i, 2 * (i // 2) - 1, 2 * (i % 2) - 1) for i in range(4)]
        c_rims = post(c_recv, [(c_send.at[i], c_recv.at[i], (a, b)) for i, a, b in ends])
        for which in range(2):
            for g in range(SIDE_TILES):
                tile = jnp.zeros((8, LANES), F32)
                for u, (c, l, row) in enumerate(ITEMS[16 * g : 16 * g + 16]):
                    first = LANE0[l] + (SIDE[l] + 3 if which else 0)
                    tile = tile + keep(turn(planes[c, row : row + 8], 8 * u - first), 8 * u, 8 * u + 6)
                    if l == 1:
                        slot, first = (8 * u, COPY0 + 2) if which else (8 * u + 3, COPY0)
                        tile = tile - keep(turn(ones_ref[c, row : row + 8], slot - first), slot, slot + 2)
                h_send[which, g] = tile
        h_rims = post(h_recv, [(h_send.at[w], h_recv.at[w], (0, 2 * w - 1)) for w in range(2)])
        for c in range(C):
            planes[c, 0:80] -= keep(ones_ref[c], 0, COPY0)

        t_cols.wait_recv()
        tops_all = gather_tops(t_send[1], t_col, "col", c_at)
        flat = [cols[FLAT_AT : FLAT_AT + LANES], cols[FLAT_AT + LANES : FLAT_AT + 2 * LANES]]
        images, mask = tops_all[0:24], tops_all[24:32]
        whole = jnp.sum(mask, axis=0, keepdims=True)
        here = whole > 0.0
        share = mask * jnp.where(here, 1.0 / jnp.where(here, whole, 1.0), 0.0)
        finer = jnp.dot(images, flat[0] + flat[1], precision=lax.Precision.HIGHEST, preferred_element_type=F32)
        detail = images - finer
        blended = [jnp.sum(detail[V * c : V * c + V] * share, axis=0, keepdims=True) for c in range(C)]
        balance = keep(jnp.sum(share, axis=0, keepdims=True) * (1.0 / V) - share, FLAT0[7], FLAT0[7] + 16)
        chain = jnp.concatenate(blended + [jnp.zeros((8 - C, LANES), F32), balance], axis=0)
        for which in range(2):
            step = jnp.dot(chain, flat[which], precision=lax.Precision.HIGHEST, preferred_element_type=F32)
            chain = chain + jnp.where(here, step, 0.0)

        for c in range(C):
            planes[c, ROW5 + 7 : ROW5 + 8] = jnp.zeros((1, LANES), F32)
        for i in range(7):
            line = keep(turn(chain, LANE5 - 7 * i), LANE5, LANE5 + 7)
            for c in range(C):
                planes[c, ROW5 + i : ROW5 + i + 1] = line[c : c + 1]
            for v in range(V):
                lines_ref[8 * v + i : 8 * v + i + 1] = line[8 + v : 9 + v]
        wide = jnp.dot(lines_ref[...], cols[128:256], precision=lax.Precision.HIGH, preferred_element_type=F32)
        for v in range(V):
            w_ref[v] = jnp.dot(
                rowc[128:256, 56:64], wide[8 * v : 8 * v + 8], precision=lax.Precision.HIGH, preferred_element_type=F32
            )

        v_rims.wait_recv()
        c_rims.wait_recv()
        h_rims.wait_recv()
        for w, a in ((1, -1), (0, 1)):
            flag = inside(a, 0)
            for c in range(C):
                for l in range(1, 5):
                    at, low = ROW0[l] + (3 if a < 0 else SIDE[l]), LANE0[l]
                    got = v_recv[w, c, HALF[l]][0:6] * flag
                    planes[c, at : at + 6] += keep(got, low, low + SIDE[l] + 9)
            for side, b in ((1, -1), (0, 1)):
                got = c_recv[2 * w + side][0:6] * inside(a, b)
                for c in range(C):
                    for l in range(1, 5):
                        at, slot = ROW0[l] + (3 if a < 0 else SIDE[l]), 8 * (4 * c + l - 1)
                        first = LANE0[l] + (3 if b < 0 else SIDE[l])
                        planes[c, at : at + 6] += keep(turn(got, first - slot), first, first + 6)
        for which, b in ((1, -1), (0, 1)):
            flag = inside(0, b)
            for i, (c, l, row) in enumerate(ITEMS):
                u = i % 16
                first = LANE0[l] + (3 if b < 0 else SIDE[l])
                got = h_recv[which, i // 16] * flag
                planes[c, row : row + 8] += keep(turn(got, first - 8 * u), first, first + 6)

        for c in range(C):
            upper = jnp.dot(rowc[0:128], planes[c, 0:128], precision=lax.Precision.HIGH, preferred_element_type=F32)
            lower = jnp.dot(rowc[128:256, 0:64], planes[c, 128:192], precision=lax.Precision.HIGH, preferred_element_type=F32)
            total = jnp.dot(upper, cols[0:128], precision=lax.Precision.HIGH, preferred_element_type=F32)
            total = total + jnp.dot(lower, cols[128:256], precision=lax.Precision.HIGH, preferred_element_type=F32)
            xs_ref[c] += total

        m_rows.wait_recv()
        means = m_send[1] + jnp.sum(m_row[...], axis=0)
        each = [jnp.broadcast_to(means[:, i : i + 1], (8, LANES)) for i in range(V * C)]
        for i in range(BLOCK // 8):
            added = [w_ref[v, 8 * i : 8 * i + 8] for v in range(V)]
            for c in range(C):
                total = xs_ref[c, 8 * i : 8 * i + 8]
                for v in range(V):
                    total = total + each[V * c + v] * added[v]
                out_ref[c, 8 * i : 8 * i + 8] = total

        for group in groups:
            group.wait_send()

    def vmem(*shape):
        return pltpu.VMEM(shape, F32)

    slabs = [vmem(n, 24, LANES) for n in (80, 48, 32, 24, 16, 16, 16)]
    wides = [vmem(ROWS[l], 24, LANES) for l in range(1, 5)]
    scratch = [
        vmem(V * C * BLOCK, LANES),
        pltpu.VMEM((N_MATS, 2 * LANES), jnp.bfloat16),
        vmem(N_COLS, LANES),
        vmem(N_ROWC, LANES),
        *slabs, *wides, *wides,
        vmem(80, 24, LANES),
        vmem(C, BLOCK, LANES),
        vmem(C, 192, LANES),
        vmem(C, 80, LANES),
        vmem(2, 1, LANES),
        vmem(nc - 1, 1, LANES),
        vmem(nr - 1, 1, LANES),
        vmem(V, LANES),
        vmem(8, V, LANES),
        vmem(2, 32, LANES),
        vmem(6, 32, LANES),
        vmem(6, 32, LANES),
        vmem(2, C, 2, 8, LANES),
        vmem(2, C, 2, 8, LANES),
        vmem(2, SIDE_TILES, 8, LANES),
        vmem(2, SIDE_TILES, 8, LANES),
        vmem(4, 8, LANES),
        vmem(4, 8, LANES),
        vmem(8 * V, LANES),
        vmem(V, BLOCK, LANES),
        pltpu.SemaphoreType.DMA((8,)),
        pltpu.SemaphoreType.DMA((8,)),
        pltpu.SemaphoreType.DMA((8,)),
        pltpu.SemaphoreType.REGULAR,
    ]
    return pl.pallas_call(
        kernel,
        out_shape=jax.ShapeDtypeStruct((C, BLOCK, BLOCK), F32),
        in_specs=[pl.BlockSpec(memory_space=pltpu.SMEM)] * 2 + [pl.BlockSpec(memory_space=pl.ANY)] * 4,
        out_specs=pl.BlockSpec(memory_space=pltpu.VMEM),
        scratch_shapes=scratch,
        compiler_params=pltpu.CompilerParams(collective_id=0, has_side_effects=True, vmem_limit_bytes=54500 << 10),
    )


def solution(mesh):
    call = make_kernel(mesh.shape["row"], mesh.shape["col"])

    def local(view_images, intersection_bits, seam_labels):
        planes = view_images.reshape(V * C * BLOCK, BLOCK)
        return call(
            intersection_bits, seam_labels, planes,
            jnp.asarray(MATS), jnp.asarray(COLS), jnp.asarray(ROWC),
        )

    placed = (P(None, None, "row", "col"), P("row", "col"), P("row", "col"))
    return jax.shard_map(local, mesh=mesh, in_specs=placed, out_specs=P(None, "row", "col"), check_vma=False)
```

```python
import numpy as np
import jax
import jax.numpy as jnp
import ml_dtypes
from jax import lax
from jax.experimental import pallas as pl
from jax.experimental.pallas import tpu as pltpu
from jax.sharding import PartitionSpec as P

V = 8
C = 3
BLOCK = 128
LANES = 128
F32 = jnp.float32
MESH = pl.DeviceIdType.MESH

SIDE = [BLOCK >> level for level in range(8)]
ROW0 = {1: 0, 2: 80, 3: 128, 4: 160}
ROWS = {1: 80, 2: 48, 3: 32, 4: 24}
LANE0 = {1: 0, 2: 80, 3: 0, 4: 32}
HALF = {1: 0, 2: 0, 3: 1, 4: 1}
ROW5, LANE5 = 184, 64
FLAT0 = {5: 0, 6: 49, 7: 74}
FLATW = {5: 7, 6: 5, 7: 4}
COPY0 = 73


def shrink_matrix(n):
    m = np.zeros((n // 2, n))
    for k in range(n // 2):
        for a, w in zip(range(-2, 3), (1.0, 4.0, 6.0, 4.0, 1.0)):
            if 0 <= 2 * k + a < n:
                m[k, 2 * k + a] += w / 16.0
    return m


def spread_matrix(n):
    m = np.zeros((2 * n, n))
    for k in range(n):
        for j, w in ((k - 1, 1 / 8), (k, 6 / 8), (k + 1, 1 / 8)):
            if 0 <= j < n:
                m[2 * k, j] += w
        for j in (k, k + 1):
            if j < n:
                m[2 * k + 1, j] += 0.5
    return m


def tile_constants():
    tiles = 10
    total = tiles * BLOCK
    down = [np.eye(total)]
    for level in range(7):
        down.append(shrink_matrix(total >> level) @ down[-1])
    step = [spread_matrix(total >> (level + 1)) for level in range(7)]
    up = [None, step[0]]
    for level in range(1, 7):
        up.append(up[-1] @ step[level])

    def rows_of(matrix, level, t, low, high):
        n = SIDE[level]
        out = np.zeros((high - low + 1, matrix.shape[1]))
        for i, k in enumerate(range(n * t + low, n * t + high + 1)):
            if 0 <= k < matrix.shape[0]:
                out[i] = matrix[k]
        return out

    mats, cols, rows = [], [], []
    for t in (0, 1, 5, 8, 9):
        here = slice(BLOCK * t, BLOCK * (t + 1))
        wide = {l: rows_of(down[l], l, t, -4, SIDE[l] + 4) for l in range(1, 5)}
        parts = {}
        for l in range(1, 5):
            span = slice(LANE0[l], LANE0[l] + SIDE[l] + 9)
            own, finer = np.zeros((BLOCK, LANES)), np.zeros((BLOCK, LANES))
            own[:, span] = wide[l][:, here].T / 16.0**l
            finer[:, span] = -rows_of(step[l] @ down[l + 1], l, t, -4, SIDE[l] + 4)[:, here].T / (8 * 16.0 ** (l + 1))
            parts[l] = np.concatenate([own, finer])
        copies = np.zeros((BLOCK, LANES))
        one = wide[1][:, here].T / 16.0
        copies[:, 3:69] = one[:, 3:69]
        copies[:, COPY0 : COPY0 + 2] = one[:, 3:5]
        copies[:, COPY0 + 2 : COPY0 + 4] = one[:, 67:69]
        column_sum, row_sum = np.zeros((1, LANES)), np.zeros((1, LANES))
        for l in (5, 6, 7):
            w, f = FLATW[l], FLAT0[l]
            local = rows_of(down[l], l, t, -1, w - 2)[:, here]
            flat = np.zeros((BLOCK, LANES))
            flat[:, f : f + w] = local.T / 16.0**l
            parts[l] = flat
            total_of = local.sum(axis=1)
            column_sum[0, f : f + w * w] = np.tile(total_of, w)
            row_sum[0, f : f + w * w] = np.repeat(total_of, w)
        high = {l: part.astype(ml_dtypes.bfloat16) for l, part in parts.items()}
        low = {l: (part - high[l].astype(np.float64)).astype(ml_dtypes.bfloat16) for l, part in parts.items()}
        copies = np.concatenate([copies, np.zeros_like(copies)]).astype(ml_dtypes.bfloat16)
        blocks = [np.concatenate([high[1], copies], axis=1), np.concatenate([low[1], np.zeros_like(copies)], axis=1)]
        blocks += [np.concatenate([high[l], low[l]], axis=1) for l in range(2, 8)]
        mats.append(np.concatenate(blocks))

        expand_a, expand_b = np.zeros((LANES, BLOCK)), np.zeros((LANES, BLOCK))
        row_a, row_b = np.zeros((BLOCK, LANES)), np.zeros((BLOCK, LANES))
        for l in range(1, 6):
            n = SIDE[l]
            for k in range(-1, n + 2):
                g = n * t + k
                if not 0 <= g < up[l].shape[1]:
                    continue
                weights = up[l][here, g]
                lane = LANE0[l] + k + 4 if l < 5 else LANE5 + k + 1
                row = ROW0[l] + k + 4 if l < 5 else ROW5 + k + 1
                if l < 3:
                    expand_a[lane] = weights
                    row_a[:, row] = weights
                else:
                    expand_b[lane] = weights
                    row_b[:, row - 128] = weights
        spread_rows, spread_lanes = np.zeros((3, 184, LANES)), np.zeros((8, LANES))
        for d in range(3):
            block = slice(BLOCK * (t + d - 1), BLOCK * (t + d))
            if not 0 <= t + d - 1 < tiles:
                continue
            for l in range(1, 5):
                share = wide[l][:, block].sum(axis=1)
                spread_rows[d, ROW0[l] : ROW0[l] + SIDE[l] + 9] = share[:, None]
                spread_lanes[2 * d + HALF[l], LANE0[l] : LANE0[l] + SIDE[l] + 9] = share
        spread_lanes[6] = column_sum
        weight_of = down[7][:, here].sum(axis=0)
        spread_lanes[7] = weight_of
        cols.append(np.concatenate([expand_a, expand_b, spread_lanes]))
        rows.append(
            np.concatenate(
                [row_a, row_b, spread_rows.reshape(-1, LANES), np.repeat(weight_of[:, None], LANES, 1), np.repeat(row_sum, 8, 0)]
            )
        )
    flat = np.zeros((2, LANES, LANES))
    for which, l in ((0, 7), (1, 6)):
        w, v = FLATW[l], FLATW[l - 1]
        local = np.zeros((v, w))
        for i in range(v):
            m, odd = divmod(i - 1, 2)
            for j, weight in ((m, 0.5), (m + 1, 0.5)) if odd else ((m - 1, 1 / 8), (m, 6 / 8), (m + 1, 1 / 8)):
                local[i, j + 1] += weight
        kron = np.einsum("ai,bj->ijab", local, local).reshape(w * w, v * v)
        flat[which, FLAT0[l] : FLAT0[l] + w * w, FLAT0[l - 1] : FLAT0[l - 1] + v * v] = kron
    cols = [np.concatenate([part, flat[0], flat[1]]) for part in cols]
    return np.stack(mats), np.stack(cols).astype(np.float32), np.stack(rows).astype(np.float32)


MATS, COLS, ROWC = tile_constants()
N_MATS, N_COLS, N_ROWC = MATS.shape[1], COLS.shape[1], ROWC.shape[1]
MATS_AT = {1: 0, 2: 512, 3: 768, 4: 1024, 5: 1280, 6: 1408, 7: 1536}
SPREAD_AT, WEIGHT_AT, RSUM_AT, FLAT_AT = 256, 808, 936, 264

AROUND = [(a, b) for a in (-1, 0, 1) for b in (-1, 0, 1) if a or b]
ITEMS = [(c, l, ROW0[l] + 8 * i) for c in range(C) for l in range(1, 5) for i in range(ROWS[l] // 8)]
ITEMS = [item for item in ITEMS if item[2] - ROW0[item[1]] <= SIDE[item[1]] + 5]
SIDE_TILES = -(-len(ITEMS) // 16)


def split(a):
    high = a.astype(jnp.bfloat16)
    return high, (a - high.astype(F32)).astype(jnp.bfloat16)


def split_dot(a, mats, l, depth):
    high, low = split(a)
    at = MATS_AT[l]
    both = jnp.dot(high, mats[at : at + depth, :], preferred_element_type=F32)
    rest = jnp.dot(low, mats[at : at + depth, :LANES], preferred_element_type=F32)
    return both[:, :LANES] + both[:, LANES:] + rest


def lanes_in(low, high, shape=(1, LANES)):
    lane = lax.broadcasted_iota(jnp.int32, shape, len(shape) - 1)
    return jnp.logical_and(lane >= low, lane < high)


def keep(value, low, high):
    return jnp.where(lanes_in(low, high), value, 0.0)


def turn(value, shift):
    shift = shift % LANES
    return pltpu.roll(value, shift, value.ndim - 1) if shift else value


def make_kernel(nr, nc):
    cells = float(nr * nc)

    def kernel(bits_ref, label_ref, x_hbm, mats_hbm, cols_hbm, rows_hbm, out_ref, *scratch):
        (x_ref, mats, cols, rowc, s1, s2, s3, s4, s5, s6, s7, e1, e2, e3, e4, d1, d2, d3, d4, copies_ref, xs_ref,
         planes, ones_ref, m_send, m_col, m_row, mask_send, mask_recv, t_send, t_packed, t_last, t_row, tp_row, tl_row, t_col, tp_col, tl_col, v_send, v_recv, h_send,
         h_recv, c_send, c_recv, lines_ref, w_ref, load_sem, send_sem, recv_sem, far_sem) = scratch
        s = {1: s1, 2: s2, 3: s3, 4: s4, 5: s5, 6: s6, 7: s7}
        e = {1: e1, 2: e2, 3: e3, 4: e4}
        d = {1: d1, 2: d2, 3: d3, 4: d4}
        r = lax.axis_index("row")
        c_at = lax.axis_index("col")

        def place(t, n):
            return jnp.where(t == 0, 0, jnp.where(t == 1, 1, jnp.where(t == n - 1, 4, jnp.where(t == n - 2, 3, 2))))

        def device(dr, dc):
            return (lax.rem(r + dr + nr, nr), lax.rem(c_at + dc + nc, nc))

        def inside(dr, dc):
            rr, cc = r + dr, c_at + dc
            ok = jnp.logical_and(jnp.logical_and(rr >= 0, rr < nr), jnp.logical_and(cc >= 0, cc < nc))
            return ok.astype(jnp.int32).astype(F32)

        row_place, col_place = place(r, nr), place(c_at, nc)
        part = V * C * BLOCK // 8
        loads = [
            pltpu.make_async_copy(
                rows_hbm.at[row_place, WEIGHT_AT : WEIGHT_AT + BLOCK], rowc.at[WEIGHT_AT : WEIGHT_AT + BLOCK], load_sem.at[0]
            ),
            pltpu.make_async_copy(cols_hbm.at[col_place, :FLAT_AT], cols.at[:FLAT_AT], load_sem.at[1]),
            pltpu.make_async_copy(mats_hbm.at[col_place], mats, load_sem.at[2]),
            pltpu.make_async_copy(rows_hbm.at[row_place, :WEIGHT_AT], rowc.at[:WEIGHT_AT], load_sem.at[3]),
            pltpu.make_async_copy(
                rows_hbm.at[row_place, WEIGHT_AT + BLOCK :], rowc.at[WEIGHT_AT + BLOCK :], load_sem.at[4]
            ),
            pltpu.make_async_copy(cols_hbm.at[col_place, FLAT_AT:], cols.at[FLAT_AT:], load_sem.at[5]),
        ]
        image_loads = [
            pltpu.make_async_copy(
                x_hbm.at[i * part : (i + 1) * part], x_ref.at[i * part : (i + 1) * part], load_sem.at[6 + i // 4]
            )
            for i in range(8)
        ]
        barrier = pltpu.get_barrier_semaphore()
        partners = [(0, i) for i in range(1, nc)] + [(i, 0) for i in (1, -1, 2, -2, 3, -3, 4, -4)]
        partners += [(a, b) for a, b in AROUND if a and b]
        loads[0].start()
        loads[1].start()
        for load in image_loads:
            load.start()
        for load in loads[2:]:
            load.start()
        for a, b in partners:
            pl.semaphore_signal(barrier, inc=1, device_id=device(a, b), device_id_type=MESH)

        groups = []

        def post(whole, copies):
            slot = len(groups)

            def describe(src, dst, to):
                return pltpu.make_async_remote_copy(
                    src_ref=src, dst_ref=dst, send_sem=send_sem.at[slot], recv_sem=recv_sem.at[slot],
                    device_id=device(*to), device_id_type=MESH,
                )

            for src, dst, to in copies:
                describe(src, dst, to).start()
            group = describe(whole, whole, copies[0][2])
            groups.append(group)
            return group

        view = lax.broadcasted_iota(jnp.int32, (V, LANES), 0)
        lane = lax.broadcasted_iota(jnp.int32, (V, LANES), 1)
        bits = jnp.full((V, LANES), bits_ref[0, 0], jnp.int32)
        label = jnp.full((V, LANES), label_ref[0, 0], jnp.int32)
        own_mask = jnp.bitwise_and(jnp.right_shift(bits, view), 1).astype(F32)
        own_mask = own_mask * jnp.where(label == view, 4.0, 1.0)
        mask_send[...] = own_mask

        for l in range(1, 8):
            n = SIDE[l]
            s[l][0:3] = jnp.zeros((3, 24, LANES), F32)
            s[l][n + 6 :] = jnp.zeros((s[l].shape[0] - n - 6, 24, LANES), F32)
        for l in range(1, 5):
            e[l][SIDE[l] + 9 :] = jnp.zeros((ROWS[l] - SIDE[l] - 9, 24, LANES), F32)
        for l, n in ((1, 75), (2, 42), (3, 25), (4, 17)):
            d[l][n:] = jnp.zeros((ROWS[l] - n, 24, LANES), F32)
        copies_ref[75:] = jnp.zeros((5, 24, LANES), F32)
        lines_ref[...] = jnp.zeros_like(lines_ref)

        loads[0].wait()
        loads[1].wait()

        weight_rows = rowc[WEIGHT_AT : WEIGHT_AT + BLOCK, :]
        weight_cols = cols[256 + 7 : 256 + 8, :]
        parts = [[] for _ in range(C)]
        for v in range(V):
            if v % 4 == 0:
                for load in image_loads[v : v + 4]:
                    load.wait()
            for c in range(C):
                weighted = x_ref[(v * C + c) * BLOCK : (v * C + c + 1) * BLOCK, :] * weight_rows
                parts[c].append(jnp.sum(weighted.reshape(16, 8, LANES), axis=0)[None])
        mean = jnp.zeros((1, LANES), F32)
        for c in range(C):
            both = jnp.sum(jnp.concatenate(parts[c], axis=0), axis=1) * weight_cols
            total = jnp.sum(both, axis=1, keepdims=True)
            mean = mean + jnp.sum(jnp.where(lane == view + V * c, total, 0.0), axis=0, keepdims=True)
        m_send[0] = mean * (1.0 / cells)

        def pixel_row(row):
            return jnp.concatenate(
                [x_ref[pl.ds(c * BLOCK + row, V, stride=C * BLOCK), :] for c in range(C)], axis=0
            )

        def tap(get, k):
            total = None
            for a, w in zip(range(-2, 3), (1.0, 4.0, 6.0, 4.0, 1.0)):
                term = get(2 * k + a)
                if term is not None:
                    term = term * w
                    total = term if total is None else total + term
            return total

        def five_taps(x):
            return (x[0] + x[4]) + 4.0 * (x[1] + x[3]) + 6.0 * x[2]

        def edge_row(row):
            return pixel_row(row) if 0 <= row < BLOCK else None

        for k in (-1, 0, 63, 64):
            s1[k + 4] = tap(edge_row, k)

        def first_pair(i, carry):
            rows = [pixel_row(4 * i + j) for j in range(7)]
            for half in range(2):
                s1[2 * i + half + 5] = five_taps(rows[2 * half :])
            return carry

        lax.fori_loop(0, 31, first_pair, 0)
        s1[69] = jnp.zeros((24, LANES), F32)
        not_first = jnp.where(r > 0, 1.0, 0.0)
        not_last = jnp.where(r < nr - 1, 1.0, 0.0)
        not_near = jnp.where(r < nr - 2, 1.0, 0.0)

        def trim(l):
            n = SIDE[l]
            s[l][3] = s[l][3] * not_first
            s[l][n + 4] = s[l][n + 4] * not_last
            s[l][n + 5] = s[l][n + 5] * (not_last if l < 7 else not_near)

        trim(1)
        for l in range(2, 8):
            n = SIDE[l]
            src, dst = s[l - 1], s[l]

            def one(i, src=src, dst=dst):
                dst[i + 3] = five_taps([src[2 * i + j] for j in range(5)])

            if l == 2:
                def five(i, carry, one=one):
                    for j in range(5):
                        one(5 * i + j)
                    return carry

                lax.fori_loop(0, 7, five, 0)
            else:
                for i in range(n + 3):
                    one(i)
            trim(l)

        pl.semaphore_wait(barrier, len(partners))
        for away in (4, -4):
            pl.semaphore_signal(far_sem, inc=1, device_id=device(away, 0), device_id_type=MESH)
        m_cols = post(m_col, [(m_send.at[0], m_col.at[i - 1], (0, i)) for i in range(1, nc)])
        masks = post(mask_recv, [(mask_send, mask_recv.at[i], to) for i, to in enumerate(AROUND)])

        for load in loads[2:]:
            load.wait()
        tops = jnp.zeros((24, LANES), F32)
        for l in (5, 6, 7):
            w = FLATW[l]
            flat_l = split_dot(s[l][3 : 3 + w].reshape(w * 24, LANES), mats, l, BLOCK).reshape(w, 24, LANES)
            for i in range(w):
                tops = tops + turn(flat_l[i], i * w)
        t_send[0, 0:24] = tops
        t_send[0, 24:32] = own_mask * (rowc[RSUM_AT : RSUM_AT + 1, :] * cols[256 + 6 : 256 + 7, :])

        def post_tops(value, recv, packed_recv, last_recv, hop):
            t_send[hop] = value
            packed = jnp.zeros((V, LANES), F32)
            last = jnp.zeros((V, LANES), F32)
            for j in range(4):
                tile = value[V * j : V * j + V]
                if j < 3:
                    packed = packed + keep(turn(tile, 41 * j - FLAT0[6]), 41 * j, 41 * j + 41)
                last = last + keep(turn(tile, 16 * j - FLAT0[7]), 16 * j, 16 * j + 16)
            t_packed[hop, 0:8] = packed
            t_packed[hop, 8:16] = value[24:32]
            t_last[hop] = last

            def to(step):
                return (step, 0) if hop == 0 else (0, step)

            return [
                post(recv, [(t_send.at[hop], recv.at[i], to(step)) for i, step in enumerate((1, -1))]),
                post(packed_recv, [(t_packed.at[hop], packed_recv.at[i], to(step)) for i, step in enumerate((2, -2))]),
                post(last_recv, [(t_last.at[hop], last_recv.at[i], to(step)) for i, step in enumerate((3, -3))]),
            ]

        t_rows = post_tops(t_send[0], t_row, tp_row, tl_row, 0)

        for l in range(1, 5):
            n, src, dst = SIDE[l], s[l + 1], e[l]

            def pair(i, src=src, dst=dst):
                x0, x1, x2 = src[i + 1], src[i + 2], src[i + 3]
                dst[2 * i] = (x0 + x2) + 6.0 * x1
                return 4.0 * (x1 + x2)

            half = n // 2 + 4
            if l < 3:
                def pairs(i, carry, pair=pair, dst=dst):
                    for j in range(4):
                        dst[2 * (4 * i + j) + 1] = pair(4 * i + j)
                    return carry

                lax.fori_loop(0, half // 4, pairs, 0)
            else:
                for i in range(half):
                    dst[2 * i + 1] = pair(i)
            dst[n + 8] = (src[half + 1] + src[half + 3]) + 6.0 * src[half + 2]

        for l, m, times in ((1, 15, 5), (2, 14, 3), (3, 25, 1), (4, 17, 1)):

            def details(i, carry, l=l, m=m):
                at = i * m
                both = jnp.concatenate(
                    [s[l][pl.ds(at, m)].reshape(m * 24, LANES), e[l][pl.ds(at, m)].reshape(m * 24, LANES)], axis=1
                )
                if l > 1:
                    d[l][pl.ds(at, m)] = split_dot(both, mats, l, 256).reshape(m, 24, LANES)
                else:
                    high, low = split(both)
                    wide = jnp.dot(high, mats[0:256, :], preferred_element_type=F32)
                    wide = wide + jnp.dot(low, mats[0:256, :], preferred_element_type=F32)
                    rest = jnp.dot(high, mats[256:512, :LANES], preferred_element_type=F32)
                    d[l][pl.ds(at, m)] = (wide[:, :LANES] + rest).reshape(m, 24, LANES)
                    copies_ref[pl.ds(at, m)] = wide[:, LANES:].reshape(m, 24, LANES)
                return carry

            if times > 1:
                lax.fori_loop(0, times, details, 0)
            else:
                details(0, 0)

        def weights(mask):
            total = jnp.sum(mask, axis=0, keepdims=True)
            return mask / jnp.where(total > 0.0, total, 1.0)

        def gather_tops(own, recv, packed_recv, last_recv, stride):
            total = own
            for i in range(2):
                for far in (1, 2, 3):
                    step = far if i else -far
                    if far == 1:
                        got = recv[i]
                    elif far == 2:
                        tiles = [turn(packed_recv[i, 0:8], FLAT0[6] - 41 * j) for j in range(3)]
                        got = jnp.concatenate(tiles + [packed_recv[i, 8:16]], axis=0)
                    else:
                        got = jnp.concatenate([turn(last_recv[i], FLAT0[7] - 16 * j) for j in range(4)], axis=0)
                    moved = None
                    for l in (5, 6, 7):
                        w, n, f = FLATW[l], SIDE[l], FLAT0[l]
                        if w <= n * far:
                            continue
                        index = lax.broadcasted_iota(jnp.int32, (1, LANES), 1) - f
                        along = index // w if stride == "row" else index % w
                        ok = lanes_in(f, f + w * w)
                        ok = jnp.logical_and(ok, jnp.logical_and(along - n * step >= 0, along - n * step < w))
                        term = jnp.where(ok, turn(got, n * step * (w if stride == "row" else 1)), 0.0)
                        moved = term if moved is None else moved + term
                    total = total + moved * (inside(step, 0) if stride == "row" else inside(0, step))
            return total

        for group in t_rows:
            group.wait_recv()
        t_cols = post_tops(gather_tops(t_send[0], t_row, tp_row, tl_row, "row"), t_col, tp_col, tl_col, 1)

        m_cols.wait_recv()
        pl.semaphore_wait(far_sem, 2)
        m_send[1] = m_send[0] + jnp.sum(m_col[...], axis=0)
        m_rows = post(m_row, [(m_send.at[1], m_row.at[i - 1], (i, 0)) for i in range(1, nr)])

        masks.wait_recv()
        around = {(0, 0): own_mask}
        for i, (a, b) in enumerate(AROUND):
            around[(-a, -b)] = mask_recv[i] * inside(-a, -b)
        inner = [
            [
                sum(around[(a, b)] * cols[256 + 2 * (b + 1) + h : 257 + 2 * (b + 1) + h, :] for b in (-1, 0, 1))
                for a in (-1, 0, 1)
            ]
            for h in range(2)
        ]

        def side_weights(a):
            left, mid, right = (weights(around[(a, b)]) for b in (-1, 0, 1))
            value = jnp.where(jnp.logical_and(lane >= COPY0, lane < COPY0 + 2), left, mid)
            return jnp.where(jnp.logical_and(lane >= COPY0 + 2, lane < COPY0 + 4), right, value)

        row_weights = {a: side_weights(a) for a in (-1, 0, 1)}

        def blend(i, l):
            at, row = i * 8, ROW0[l] + i * 8
            if not isinstance(i, int):
                at, row = pl.multiple_of(at, 8), pl.multiple_of(row, 8)
            mask = None
            for a in range(3):
                term = rowc[pl.ds(SPREAD_AT + 184 * a + row, 8), :][:, None, :] * inner[HALF[l]][a][None]
                mask = term if mask is None else mask + term
            whole = jnp.sum(mask, axis=1)
            inverse = jnp.where(whole > 0.0, 1.0 / jnp.where(whole > 0.0, whole, 1.0), 0.0)
            for c in range(C):
                part = d[l][pl.ds(at, 8), V * c : V * c + V, :]
                planes[c, pl.ds(row, 8), :] = jnp.sum(part * mask, axis=1) * inverse
                if l == 1:
                    part = copies_ref[pl.ds(at, 8), V * c : V * c + V, :]
                    ones_ref[c, pl.ds(at, 8), :] = jnp.sum(part * row_weights[0][None], axis=1)

        def blend_rest(i, carry, l):
            blend(i, l)
            return carry

        for l, blocks in ((1, (0, 8, 9)), (2, (0, 4, 5)), (3, (0, 2, 3)), (4, (0, 1, 2))):
            for i in blocks:
                blend(i, l)

        for w in range(2):
            corners = [jnp.zeros((8, LANES), F32) for _ in range(2)]
            for c in range(C):
                at = {l: ROW0[l] + (SIDE[l] + 3 if w else 0) for l in range(1, 5)}
                halves = [planes[c, at[l] : at[l] + 8] + planes[c, at[l + 1] : at[l + 1] + 8] for l in (1, 3)]
                one = copies_ref[at[1] : at[1] + 8, V * c : V * c + V, :]
                one = jnp.sum(one * row_weights[1 if w else -1][None], axis=1)
                v_send[w, c, 0] = halves[0] - keep(one, 0, COPY0)
                v_send[w, c, 1] = halves[1]
                for side in range(2):
                    for l in range(1, 5):
                        slot = 8 * (4 * c + l - 1)
                        first = LANE0[l] + (SIDE[l] + 3 if side else 0)
                        corners[side] += keep(turn(halves[HALF[l]], slot - first), slot, slot + 6)
                    slot, first = (32 * c, COPY0 + 2) if side else (32 * c + 3, COPY0)
                    corners[side] -= keep(turn(one, slot - first), slot, slot + 2)
            for side in range(2):
                c_send[2 * w + side] = corners[side]
        v_rims = post(v_recv, [(v_send.at[w], v_recv.at[w], (2 * w - 1, 0)) for w in range(2)])
        ends = [(i, 2 * (i // 2) - 1, 2 * (i % 2) - 1) for i in range(4)]
        c_rims = post(c_recv, [(c_send.at[i], c_recv.at[i], (a, b)) for i, a, b in ends])
        for l, first, last in ((1, 1, 8), (2, 1, 4), (3, 1, 2)):
            lax.fori_loop(first, last, lambda i, carry, l=l: blend_rest(i, carry, l), 0)
        for which in range(2):
            for g in range(SIDE_TILES):
                tile = jnp.zeros((8, LANES), F32)
                for u, (c, l, row) in enumerate(ITEMS[16 * g : 16 * g + 16]):
                    first = LANE0[l] + (SIDE[l] + 3 if which else 0)
                    tile = tile + keep(turn(planes[c, row : row + 8], 8 * u - first), 8 * u, 8 * u + 6)
                    if l == 1:
                        slot, first = (8 * u, COPY0 + 2) if which else (8 * u + 3, COPY0)
                        tile = tile - keep(turn(ones_ref[c, row : row + 8], slot - first), slot, slot + 2)
                h_send[which, g] = tile
        h_rims = post(h_recv, [(h_send.at[w], h_recv.at[w], (0, 2 * w - 1)) for w in range(2)])
        for c in range(C):
            planes[c, 0:80] -= keep(ones_ref[c], 0, COPY0)

        own_weights = weights(own_mask)
        for c in range(C):
            total = None
            for v in range(V):
                term = x_ref[(v * C + c) * BLOCK : (v * C + c + 1) * BLOCK, :] * own_weights[v : v + 1, :]
                total = term if total is None else total + term
            xs_ref[c] = total

        for group in t_cols:
            group.wait_recv()
        tops_all = gather_tops(t_send[1], t_col, tp_col, tl_col, "col")
        flat = [cols[FLAT_AT : FLAT_AT + LANES], cols[FLAT_AT + LANES : FLAT_AT + 2 * LANES]]
        images, mask = tops_all[0:24], tops_all[24:32]
        whole = jnp.sum(mask, axis=0, keepdims=True)
        here = whole > 0.0
        share = mask * jnp.where(here, 1.0 / jnp.where(here, whole, 1.0), 0.0)
        finer = jnp.dot(images, flat[0] + flat[1], precision=lax.Precision.HIGHEST, preferred_element_type=F32)
        detail = images - finer
        blended = [jnp.sum(detail[V * c : V * c + V] * share, axis=0, keepdims=True) for c in range(C)]
        balance = keep(jnp.sum(share, axis=0, keepdims=True) * (1.0 / V) - share, FLAT0[7], FLAT0[7] + 16)
        chain = jnp.concatenate(blended + [jnp.zeros((8 - C, LANES), F32), balance], axis=0)
        for which in range(2):
            step = jnp.dot(chain, flat[which], precision=lax.Precision.HIGHEST, preferred_element_type=F32)
            chain = chain + jnp.where(here, step, 0.0)

        for c in range(C):
            planes[c, ROW5 + 7 : ROW5 + 8] = jnp.zeros((1, LANES), F32)
        for i in range(7):
            line = keep(turn(chain, LANE5 - 7 * i), LANE5, LANE5 + 7)
            for c in range(C):
                planes[c, ROW5 + i : ROW5 + i + 1] = line[c : c + 1]
            for v in range(V):
                lines_ref[8 * v + i : 8 * v + i + 1] = line[8 + v : 9 + v]
        wide = jnp.dot(lines_ref[...], cols[128:256], precision=lax.Precision.HIGH, preferred_element_type=F32)
        for v in range(V):
            w_ref[v] = jnp.dot(
                rowc[128:256, 56:64], wide[8 * v : 8 * v + 8], precision=lax.Precision.HIGH, preferred_element_type=F32
            )

        v_rims.wait_recv()
        c_rims.wait_recv()
        h_rims.wait_recv()
        for w, a in ((1, -1), (0, 1)):
            flag = inside(a, 0)
            for c in range(C):
                for l in range(1, 5):
                    at, low = ROW0[l] + (3 if a < 0 else SIDE[l]), LANE0[l]
                    got = v_recv[w, c, HALF[l]][0:6] * flag
                    planes[c, at : at + 6] += keep(got, low, low + SIDE[l] + 9)
            for side, b in ((1, -1), (0, 1)):
                got = c_recv[2 * w + side][0:6] * inside(a, b)
                for c in range(C):
                    for l in range(1, 5):
                        at, slot = ROW0[l] + (3 if a < 0 else SIDE[l]), 8 * (4 * c + l - 1)
                        first = LANE0[l] + (3 if b < 0 else SIDE[l])
                        planes[c, at : at + 6] += keep(turn(got, first - slot), first, first + 6)
        for which, b in ((1, -1), (0, 1)):
            flag = inside(0, b)
            for i, (c, l, row) in enumerate(ITEMS):
                u = i % 16
                first = LANE0[l] + (3 if b < 0 else SIDE[l])
                got = h_recv[which, i // 16] * flag
                planes[c, row : row + 8] += keep(turn(got, first - 8 * u), first, first + 6)

        def wide_dot(a, b):
            return jnp.dot(a, b, precision=lax.Precision.HIGH, preferred_element_type=F32)

        upper = wide_dot(jnp.concatenate([planes[c, 0:128] for c in range(C)], axis=0), cols[0:128])
        lower = wide_dot(jnp.concatenate([planes[c, 128:192] for c in range(C)], axis=0), cols[128:256])
        across = [jnp.concatenate([upper[128 * c : 128 * c + 128], lower[64 * c : 64 * c + 64]], axis=0) for c in range(C)]
        total = wide_dot(
            jnp.concatenate([rowc[0:128], rowc[128:256]], axis=1)[:, 0:192], jnp.concatenate(across, axis=1)
        )
        for c in range(C):
            xs_ref[c] += total[:, LANES * c : LANES * c + LANES]

        m_rows.wait_recv()
        means = m_send[1] + jnp.sum(m_row[...], axis=0)
        each = [jnp.broadcast_to(means[:, i : i + 1], (8, LANES)) for i in range(V * C)]
        for i in range(BLOCK // 8):
            added = [w_ref[v, 8 * i : 8 * i + 8] for v in range(V)]
            for c in range(C):
                total = xs_ref[c, 8 * i : 8 * i + 8]
                for v in range(V):
                    total = total + each[V * c + v] * added[v]
                out_ref[c, 8 * i : 8 * i + 8] = total

        for group in groups:
            group.wait_send()

    def vmem(*shape):
        return pltpu.VMEM(shape, F32)

    slabs = [vmem(n, 24, LANES) for n in (80, 48, 32, 24, 16, 16, 16)]
    wides = [vmem(ROWS[l], 24, LANES) for l in range(1, 5)]
    scratch = [
        vmem(V * C * BLOCK, LANES),
        pltpu.VMEM((N_MATS, 2 * LANES), jnp.bfloat16),
        vmem(N_COLS, LANES),
        vmem(N_ROWC, LANES),
        *slabs, *wides, *wides,
        vmem(80, 24, LANES),
        vmem(C, BLOCK, LANES),
        vmem(C, 192, LANES),
        vmem(C, 80, LANES),
        vmem(2, 1, LANES),
        vmem(nc - 1, 1, LANES),
        vmem(nr - 1, 1, LANES),
        vmem(V, LANES),
        vmem(8, V, LANES),
        vmem(2, 32, LANES),
        vmem(2, 16, LANES),
        vmem(2, 8, LANES),
        *[vmem(2, n, LANES) for n in (32, 16, 8, 32, 16, 8)],
        vmem(2, C, 2, 8, LANES),
        vmem(2, C, 2, 8, LANES),
        vmem(2, SIDE_TILES, 8, LANES),
        vmem(2, SIDE_TILES, 8, LANES),
        vmem(4, 8, LANES),
        vmem(4, 8, LANES),
        vmem(8 * V, LANES),
        vmem(V, BLOCK, LANES),
        pltpu.SemaphoreType.DMA((8,)),
        pltpu.SemaphoreType.DMA((12,)),
        pltpu.SemaphoreType.DMA((12,)),
        pltpu.SemaphoreType.REGULAR,
    ]
    return pl.pallas_call(
        kernel,
        out_shape=jax.ShapeDtypeStruct((C, BLOCK, BLOCK), F32),
        in_specs=[pl.BlockSpec(memory_space=pltpu.SMEM)] * 2 + [pl.BlockSpec(memory_space=pl.ANY)] * 4,
        out_specs=pl.BlockSpec(memory_space=pltpu.VMEM),
        scratch_shapes=scratch,
        compiler_params=pltpu.CompilerParams(collective_id=0, has_side_effects=True, vmem_limit_bytes=54500 << 10),
    )


def solution(mesh):
    call = make_kernel(mesh.shape["row"], mesh.shape["col"])

    def local(view_images, intersection_bits, seam_labels):
        planes = view_images.reshape(V * C * BLOCK, BLOCK)
        return call(
            intersection_bits, seam_labels, planes,
            jnp.asarray(MATS), jnp.asarray(COLS), jnp.asarray(ROWC),
        )

    placed = (P(None, None, "row", "col"), P("row", "col"), P("row", "col"))
    return jax.shard_map(local, mesh=mesh, in_specs=placed, out_specs=P(None, "row", "col"), check_vma=False)
```

```python
import numpy as np
import jax
import jax.numpy as jnp
import ml_dtypes
from jax import lax
from jax.experimental import pallas as pl
from jax.experimental.pallas import tpu as pltpu
from jax.sharding import PartitionSpec as P

V = 8
C = 3
BLOCK = 128
LANES = 128
F32 = jnp.float32
MESH = pl.DeviceIdType.MESH

SIDE = [BLOCK >> level for level in range(8)]
ROW0 = {1: 0, 2: 80, 3: 128, 4: 160}
ROWS = {1: 80, 2: 48, 3: 32, 4: 24}
LANE0 = {1: 0, 2: 80, 3: 0, 4: 32}
HALF = {1: 0, 2: 0, 3: 1, 4: 1}
ROW5, LANE5 = 184, 64
FLAT0 = {5: 0, 6: 49, 7: 74}
FLATW = {5: 7, 6: 5, 7: 4}
COPY0 = 73


def shrink_matrix(n):
    m = np.zeros((n // 2, n))
    for k in range(n // 2):
        for a, w in zip(range(-2, 3), (1.0, 4.0, 6.0, 4.0, 1.0)):
            if 0 <= 2 * k + a < n:
                m[k, 2 * k + a] += w / 16.0
    return m


def spread_matrix(n):
    m = np.zeros((2 * n, n))
    for k in range(n):
        for j, w in ((k - 1, 1 / 8), (k, 6 / 8), (k + 1, 1 / 8)):
            if 0 <= j < n:
                m[2 * k, j] += w
        for j in (k, k + 1):
            if j < n:
                m[2 * k + 1, j] += 0.5
    return m


def tile_constants():
    tiles = 10
    total = tiles * BLOCK
    down = [np.eye(total)]
    for level in range(7):
        down.append(shrink_matrix(total >> level) @ down[-1])
    step = [spread_matrix(total >> (level + 1)) for level in range(7)]
    up = [None, step[0]]
    for level in range(1, 7):
        up.append(up[-1] @ step[level])

    def rows_of(matrix, level, t, low, high):
        n = SIDE[level]
        out = np.zeros((high - low + 1, matrix.shape[1]))
        for i, k in enumerate(range(n * t + low, n * t + high + 1)):
            if 0 <= k < matrix.shape[0]:
                out[i] = matrix[k]
        return out

    mats, cols, rows = [], [], []
    for t in (0, 1, 5, 8, 9):
        here = slice(BLOCK * t, BLOCK * (t + 1))
        wide = {l: rows_of(down[l], l, t, -4, SIDE[l] + 4) for l in range(1, 5)}
        parts = {}
        for l in range(1, 5):
            span = slice(LANE0[l], LANE0[l] + SIDE[l] + 9)
            own, finer = np.zeros((BLOCK, LANES)), np.zeros((BLOCK, LANES))
            own[:, span] = wide[l][:, here].T / 16.0**l
            finer[:, span] = -rows_of(step[l] @ down[l + 1], l, t, -4, SIDE[l] + 4)[:, here].T / (8 * 16.0 ** (l + 1))
            parts[l] = np.concatenate([own, finer])
        copies = np.zeros((BLOCK, LANES))
        one = wide[1][:, here].T / 16.0
        copies[:, 3:69] = one[:, 3:69]
        copies[:, COPY0 : COPY0 + 2] = one[:, 3:5]
        copies[:, COPY0 + 2 : COPY0 + 4] = one[:, 67:69]
        column_sum, row_sum = np.zeros((1, LANES)), np.zeros((1, LANES))
        for l in (5, 6, 7):
            w, f = FLATW[l], FLAT0[l]
            local = rows_of(down[l], l, t, -1, w - 2)[:, here]
            flat = np.zeros((BLOCK, LANES))
            flat[:, f : f + w] = local.T / 16.0**l
            parts[l] = flat
            total_of = local.sum(axis=1)
            column_sum[0, f : f + w * w] = np.tile(total_of, w)
            row_sum[0, f : f + w * w] = np.repeat(total_of, w)
        high = {l: part.astype(ml_dtypes.bfloat16) for l, part in parts.items()}
        low = {l: (part - high[l].astype(np.float64)).astype(ml_dtypes.bfloat16) for l, part in parts.items()}
        copies = np.concatenate([copies, np.zeros_like(copies)]).astype(ml_dtypes.bfloat16)
        blocks = [np.concatenate([high[1], copies], axis=1), np.concatenate([low[1], np.zeros_like(copies)], axis=1)]
        blocks += [np.concatenate([high[l], low[l]], axis=1) for l in range(2, 8)]
        mats.append(np.concatenate(blocks))

        expand_a, expand_b = np.zeros((LANES, BLOCK)), np.zeros((LANES, BLOCK))
        row_a, row_b = np.zeros((BLOCK, LANES)), np.zeros((BLOCK, LANES))
        for l in range(1, 6):
            n = SIDE[l]
            for k in range(-1, n + 2):
                g = n * t + k
                if not 0 <= g < up[l].shape[1]:
                    continue
                weights = up[l][here, g]
                lane = LANE0[l] + k + 4 if l < 5 else LANE5 + k + 1
                row = ROW0[l] + k + 4 if l < 5 else ROW5 + k + 1
                if l < 3:
                    expand_a[lane] = weights
                    row_a[:, row] = weights
                else:
                    expand_b[lane] = weights
                    row_b[:, row - 128] = weights
        spread_rows, spread_lanes = np.zeros((3, 184, LANES)), np.zeros((8, LANES))
        for d in range(3):
            block = slice(BLOCK * (t + d - 1), BLOCK * (t + d))
            if not 0 <= t + d - 1 < tiles:
                continue
            for l in range(1, 5):
                share = wide[l][:, block].sum(axis=1)
                spread_rows[d, ROW0[l] : ROW0[l] + SIDE[l] + 9] = share[:, None]
                spread_lanes[2 * d + HALF[l], LANE0[l] : LANE0[l] + SIDE[l] + 9] = share
        spread_lanes[6] = column_sum
        weight_of = down[7][:, here].sum(axis=0)
        spread_lanes[7] = weight_of
        cols.append(np.concatenate([expand_a, expand_b, spread_lanes]))
        rows.append(
            np.concatenate(
                [row_a, row_b, spread_rows.reshape(-1, LANES), np.repeat(weight_of[:, None], LANES, 1), np.repeat(row_sum, 8, 0)]
            )
        )
    flat = np.zeros((2, LANES, LANES))
    for which, l in ((0, 7), (1, 6)):
        w, v = FLATW[l], FLATW[l - 1]
        local = np.zeros((v, w))
        for i in range(v):
            m, odd = divmod(i - 1, 2)
            for j, weight in ((m, 0.5), (m + 1, 0.5)) if odd else ((m - 1, 1 / 8), (m, 6 / 8), (m + 1, 1 / 8)):
                local[i, j + 1] += weight
        kron = np.einsum("ai,bj->ijab", local, local).reshape(w * w, v * v)
        flat[which, FLAT0[l] : FLAT0[l] + w * w, FLAT0[l - 1] : FLAT0[l - 1] + v * v] = kron
    def flattened(part):
        out = np.zeros((LANES, LANES))
        for i in range(7):
            out[7 * i : 7 * i + 7] = part[128 + LANE5 : 128 + LANE5 + 7]
        return out

    cols = [np.concatenate([part, flat[0], flat[1], flattened(part)]) for part in cols]
    return np.stack(mats), np.stack(cols).astype(np.float32), np.stack(rows).astype(np.float32)


MATS, COLS, ROWC = tile_constants()
N_MATS, N_COLS, N_ROWC = MATS.shape[1], COLS.shape[1], ROWC.shape[1]
MATS_AT = {1: 0, 2: 512, 3: 768, 4: 1024, 5: 1280, 6: 1408, 7: 1536}
SPREAD_AT, WEIGHT_AT, RSUM_AT, FLAT_AT = 256, 808, 936, 264

AROUND = [(a, b) for a in (-1, 0, 1) for b in (-1, 0, 1) if a or b]
ITEMS = [(c, l, ROW0[l] + 8 * i) for c in range(C) for l in range(1, 5) for i in range(ROWS[l] // 8)]
ITEMS = [item for item in ITEMS if item[2] - ROW0[item[1]] <= SIDE[item[1]] + 5]
SIDE_TILES = -(-len(ITEMS) // 16)


def split(a):
    high = a.astype(jnp.bfloat16)
    return high, (a - high.astype(F32)).astype(jnp.bfloat16)


def split_dot(a, mats, l, depth):
    high, low = split(a)
    at = MATS_AT[l]
    both = jnp.dot(high, mats[at : at + depth, :], preferred_element_type=F32)
    rest = jnp.dot(low, mats[at : at + depth, :LANES], preferred_element_type=F32)
    return both[:, :LANES] + both[:, LANES:] + rest


def lanes_in(low, high, shape=(1, LANES)):
    lane = lax.broadcasted_iota(jnp.int32, shape, len(shape) - 1)
    return jnp.logical_and(lane >= low, lane < high)


def keep(value, low, high):
    return jnp.where(lanes_in(low, high), value, 0.0)


def turn(value, shift):
    shift = shift % LANES
    return pltpu.roll(value, shift, value.ndim - 1) if shift else value


def make_kernel(nr, nc):
    cells = float(nr * nc)

    def kernel(bits_ref, label_ref, x_hbm, mats_hbm, cols_hbm, rows_hbm, out_ref, *scratch):
        (x_ref, mats, cols, rowc, s1, s2, s3, s4, s5, s6, s7, e1, e2, e3, e4, d1, d2, d3, d4, copies_ref, xs_ref,
         planes, ones_ref, m_send, m_col, m_row, mask_send, mask_recv, t_send, t_packed, t_last, t_row, tp_row, tl_row, t_col, tp_col, tl_col, v_send, v_recv, h_send,
         h_recv, c_send, c_recv, w_ref, load_sem, send_sem, recv_sem, far_sem) = scratch
        s = {1: s1, 2: s2, 3: s3, 4: s4, 5: s5, 6: s6, 7: s7}
        e = {1: e1, 2: e2, 3: e3, 4: e4}
        d = {1: d1, 2: d2, 3: d3, 4: d4}
        r = lax.axis_index("row")
        c_at = lax.axis_index("col")

        def place(t, n):
            return jnp.where(t == 0, 0, jnp.where(t == 1, 1, jnp.where(t == n - 1, 4, jnp.where(t == n - 2, 3, 2))))

        def device(dr, dc):
            return (lax.rem(r + dr + nr, nr), lax.rem(c_at + dc + nc, nc))

        def inside(dr, dc):
            rr, cc = r + dr, c_at + dc
            ok = jnp.logical_and(jnp.logical_and(rr >= 0, rr < nr), jnp.logical_and(cc >= 0, cc < nc))
            return ok.astype(jnp.int32).astype(F32)

        row_place, col_place = place(r, nr), place(c_at, nc)
        part = V * C * BLOCK // 8
        loads = [
            pltpu.make_async_copy(
                rows_hbm.at[row_place, WEIGHT_AT : WEIGHT_AT + BLOCK], rowc.at[WEIGHT_AT : WEIGHT_AT + BLOCK], load_sem.at[0]
            ),
            pltpu.make_async_copy(cols_hbm.at[col_place, :FLAT_AT], cols.at[:FLAT_AT], load_sem.at[1]),
            pltpu.make_async_copy(mats_hbm.at[col_place], mats, load_sem.at[2]),
            pltpu.make_async_copy(rows_hbm.at[row_place, :WEIGHT_AT], rowc.at[:WEIGHT_AT], load_sem.at[3]),
            pltpu.make_async_copy(
                rows_hbm.at[row_place, WEIGHT_AT + BLOCK :], rowc.at[WEIGHT_AT + BLOCK :], load_sem.at[4]
            ),
            pltpu.make_async_copy(cols_hbm.at[col_place, FLAT_AT:], cols.at[FLAT_AT:], load_sem.at[5]),
        ]
        image_loads = [
            pltpu.make_async_copy(
                x_hbm.at[i * part : (i + 1) * part], x_ref.at[i * part : (i + 1) * part], load_sem.at[6 + i // 4]
            )
            for i in range(8)
        ]
        barrier = pltpu.get_barrier_semaphore()
        partners = [(0, i) for i in range(1, nc)] + [(i, 0) for i in (1, -1, 2, -2, 3, -3, 4, -4)]
        partners += [(a, b) for a, b in AROUND if a and b]
        loads[0].start()
        loads[1].start()
        for load in image_loads:
            load.start()
        for load in loads[2:]:
            load.start()
        for a, b in partners:
            pl.semaphore_signal(barrier, inc=1, device_id=device(a, b), device_id_type=MESH)

        groups = []

        def post(whole, copies):
            slot = len(groups)

            def describe(src, dst, to):
                return pltpu.make_async_remote_copy(
                    src_ref=src, dst_ref=dst, send_sem=send_sem.at[slot], recv_sem=recv_sem.at[slot],
                    device_id=device(*to), device_id_type=MESH,
                )

            for src, dst, to in copies:
                describe(src, dst, to).start()
            group = describe(whole, whole, copies[0][2])
            groups.append(group)
            return group

        view = lax.broadcasted_iota(jnp.int32, (V, LANES), 0)
        lane = lax.broadcasted_iota(jnp.int32, (V, LANES), 1)
        bits = jnp.full((V, LANES), bits_ref[0, 0], jnp.int32)
        label = jnp.full((V, LANES), label_ref[0, 0], jnp.int32)
        own_mask = jnp.bitwise_and(jnp.right_shift(bits, view), 1).astype(F32)
        own_mask = own_mask * jnp.where(label == view, 4.0, 1.0)
        mask_send[...] = own_mask

        for l in range(1, 8):
            n = SIDE[l]
            s[l][0:3] = jnp.zeros((3, 24, LANES), F32)
            s[l][n + 6 :] = jnp.zeros((s[l].shape[0] - n - 6, 24, LANES), F32)
        for l in range(1, 5):
            e[l][SIDE[l] + 9 :] = jnp.zeros((ROWS[l] - SIDE[l] - 9, 24, LANES), F32)
        for l, n in ((1, 75), (2, 42), (3, 25), (4, 17)):
            d[l][n:] = jnp.zeros((ROWS[l] - n, 24, LANES), F32)
        copies_ref[75:] = jnp.zeros((5, 24, LANES), F32)
        planes[:, ROW5:] = jnp.zeros((C, 192 - ROW5, LANES), F32)

        loads[0].wait()
        loads[1].wait()

        weight_rows = rowc[WEIGHT_AT : WEIGHT_AT + BLOCK, :]
        weight_cols = cols[256 + 7 : 256 + 8, :]
        parts = [[] for _ in range(C)]
        for v in range(V):
            if v % 4 == 0:
                for load in image_loads[v : v + 4]:
                    load.wait()
            for c in range(C):
                weighted = x_ref[(v * C + c) * BLOCK : (v * C + c + 1) * BLOCK, :] * weight_rows
                parts[c].append(jnp.sum(weighted.reshape(16, 8, LANES), axis=0)[None])
        mean = jnp.zeros((1, LANES), F32)
        for c in range(C):
            both = jnp.sum(jnp.concatenate(parts[c], axis=0), axis=1) * weight_cols
            total = jnp.sum(both, axis=1, keepdims=True)
            mean = mean + jnp.sum(jnp.where(lane == view + V * c, total, 0.0), axis=0, keepdims=True)
        m_send[0] = mean * (1.0 / cells)

        def pixel_row(row):
            return jnp.concatenate(
                [x_ref[pl.ds(c * BLOCK + row, V, stride=C * BLOCK), :] for c in range(C)], axis=0
            )

        def tap(get, k):
            total = None
            for a, w in zip(range(-2, 3), (1.0, 4.0, 6.0, 4.0, 1.0)):
                term = get(2 * k + a)
                if term is not None:
                    term = term * w
                    total = term if total is None else total + term
            return total

        def five_taps(x):
            return (x[0] + x[4]) + 4.0 * (x[1] + x[3]) + 6.0 * x[2]

        def edge_row(row):
            return pixel_row(row) if 0 <= row < BLOCK else None

        for k in (-1, 0, 63, 64):
            s1[k + 4] = tap(edge_row, k)

        def first_pair(i, carry):
            rows = [pixel_row(4 * i + j) for j in range(7)]
            for half in range(2):
                s1[2 * i + half + 5] = five_taps(rows[2 * half :])
            return carry

        lax.fori_loop(0, 31, first_pair, 0)
        s1[69] = jnp.zeros((24, LANES), F32)
        not_first = jnp.where(r > 0, 1.0, 0.0)
        not_last = jnp.where(r < nr - 1, 1.0, 0.0)
        not_near = jnp.where(r < nr - 2, 1.0, 0.0)

        def trim(l):
            n = SIDE[l]
            s[l][3] = s[l][3] * not_first
            s[l][n + 4] = s[l][n + 4] * not_last
            s[l][n + 5] = s[l][n + 5] * (not_last if l < 7 else not_near)

        trim(1)
        for l in range(2, 8):
            n = SIDE[l]
            src, dst = s[l - 1], s[l]

            def one(i, src=src, dst=dst):
                dst[i + 3] = five_taps([src[2 * i + j] for j in range(5)])

            if l == 2:
                def five(i, carry, one=one):
                    for j in range(5):
                        one(5 * i + j)
                    return carry

                lax.fori_loop(0, 7, five, 0)
            else:
                for i in range(n + 3):
                    one(i)
            trim(l)

        pl.semaphore_wait(barrier, len(partners))
        for away in (4, -4):
            pl.semaphore_signal(far_sem, inc=1, device_id=device(away, 0), device_id_type=MESH)
        m_cols = post(m_col, [(m_send.at[0], m_col.at[i - 1], (0, i)) for i in range(1, nc)])
        masks = post(mask_recv, [(mask_send, mask_recv.at[i], to) for i, to in enumerate(AROUND)])

        for load in loads[2:]:
            load.wait()
        tops = jnp.zeros((24, LANES), F32)
        for l in (5, 6, 7):
            w = FLATW[l]
            flat_l = split_dot(s[l][3 : 3 + w].reshape(w * 24, LANES), mats, l, BLOCK).reshape(w, 24, LANES)
            for i in range(w):
                tops = tops + turn(flat_l[i], i * w)
        t_send[0, 0:24] = tops
        t_send[0, 24:32] = own_mask * (rowc[RSUM_AT : RSUM_AT + 1, :] * cols[256 + 6 : 256 + 7, :])

        def post_tops(value, recv, packed_recv, last_recv, hop):
            t_send[hop] = value
            packed = jnp.zeros((V, LANES), F32)
            last = jnp.zeros((V, LANES), F32)
            for j in range(4):
                tile = value[V * j : V * j + V]
                if j < 3:
                    packed = packed + keep(turn(tile, 41 * j - FLAT0[6]), 41 * j, 41 * j + 41)
                last = last + keep(turn(tile, 16 * j - FLAT0[7]), 16 * j, 16 * j + 16)
            t_packed[hop, 0:8] = packed
            t_packed[hop, 8:16] = value[24:32]
            t_last[hop] = last

            def to(step):
                return (step, 0) if hop == 0 else (0, step)

            return [
                post(recv, [(t_send.at[hop], recv.at[i], to(step)) for i, step in enumerate((1, -1))]),
                post(packed_recv, [(t_packed.at[hop], packed_recv.at[i], to(step)) for i, step in enumerate((2, -2))]),
                post(last_recv, [(t_last.at[hop], last_recv.at[i], to(step)) for i, step in enumerate((3, -3))]),
            ]

        t_rows = post_tops(t_send[0], t_row, tp_row, tl_row, 0)

        for l in range(1, 5):
            n, src, dst = SIDE[l], s[l + 1], e[l]

            def pair(i, src=src, dst=dst):
                x0, x1, x2 = src[i + 1], src[i + 2], src[i + 3]
                dst[2 * i] = (x0 + x2) + 6.0 * x1
                return 4.0 * (x1 + x2)

            half = n // 2 + 4
            if l < 3:
                def pairs(i, carry, pair=pair, dst=dst):
                    for j in range(4):
                        dst[2 * (4 * i + j) + 1] = pair(4 * i + j)
                    return carry

                lax.fori_loop(0, half // 4, pairs, 0)
            else:
                for i in range(half):
                    dst[2 * i + 1] = pair(i)
            dst[n + 8] = (src[half + 1] + src[half + 3]) + 6.0 * src[half + 2]

        for l, m, times in ((1, 15, 5), (2, 14, 3), (3, 25, 1), (4, 17, 1)):

            def details(i, carry, l=l, m=m):
                at = i * m
                both = jnp.concatenate(
                    [s[l][pl.ds(at, m)].reshape(m * 24, LANES), e[l][pl.ds(at, m)].reshape(m * 24, LANES)], axis=1
                )
                if l > 1:
                    d[l][pl.ds(at, m)] = split_dot(both, mats, l, 256).reshape(m, 24, LANES)
                else:
                    high, low = split(both)
                    wide = jnp.dot(high, mats[0:256, :], preferred_element_type=F32)
                    wide = wide + jnp.dot(low, mats[0:256, :], preferred_element_type=F32)
                    rest = jnp.dot(high, mats[256:512, :LANES], preferred_element_type=F32)
                    d[l][pl.ds(at, m)] = (wide[:, :LANES] + rest).reshape(m, 24, LANES)
                    copies_ref[pl.ds(at, m)] = wide[:, LANES:].reshape(m, 24, LANES)
                return carry

            if times > 1:
                lax.fori_loop(0, times, details, 0)
            else:
                details(0, 0)

        def weights(mask):
            total = jnp.sum(mask, axis=0, keepdims=True)
            return mask / jnp.where(total > 0.0, total, 1.0)

        def gather_tops(own, recv, packed_recv, last_recv, stride):
            total = own
            for i in range(2):
                for far in (1, 2, 3):
                    step = far if i else -far
                    if far == 1:
                        got = recv[i]
                    elif far == 2:
                        tiles = [turn(packed_recv[i, 0:8], FLAT0[6] - 41 * j) for j in range(3)]
                        got = jnp.concatenate(tiles + [packed_recv[i, 8:16]], axis=0)
                    else:
                        got = jnp.concatenate([turn(last_recv[i], FLAT0[7] - 16 * j) for j in range(4)], axis=0)
                    moved = None
                    for l in (5, 6, 7):
                        w, n, f = FLATW[l], SIDE[l], FLAT0[l]
                        if w <= n * far:
                            continue
                        index = lax.broadcasted_iota(jnp.int32, (1, LANES), 1) - f
                        along = index // w if stride == "row" else index % w
                        ok = lanes_in(f, f + w * w)
                        ok = jnp.logical_and(ok, jnp.logical_and(along - n * step >= 0, along - n * step < w))
                        term = jnp.where(ok, turn(got, n * step * (w if stride == "row" else 1)), 0.0)
                        moved = term if moved is None else moved + term
                    total = total + moved * (inside(step, 0) if stride == "row" else inside(0, step))
            return total

        for group in t_rows:
            group.wait_recv()
        t_cols = post_tops(gather_tops(t_send[0], t_row, tp_row, tl_row, "row"), t_col, tp_col, tl_col, 1)

        m_cols.wait_recv()
        pl.semaphore_wait(far_sem, 2)
        m_send[1] = m_send[0] + jnp.sum(m_col[...], axis=0)
        m_rows = post(m_row, [(m_send.at[1], m_row.at[i - 1], (i, 0)) for i in range(1, nr)])

        masks.wait_recv()
        around = {(0, 0): own_mask}
        for i, (a, b) in enumerate(AROUND):
            around[(-a, -b)] = mask_recv[i] * inside(-a, -b)
        inner = [
            [
                sum(around[(a, b)] * cols[256 + 2 * (b + 1) + h : 257 + 2 * (b + 1) + h, :] for b in (-1, 0, 1))
                for a in (-1, 0, 1)
            ]
            for h in range(2)
        ]

        def side_weights(a):
            left, mid, right = (weights(around[(a, b)]) for b in (-1, 0, 1))
            value = jnp.where(jnp.logical_and(lane >= COPY0, lane < COPY0 + 2), left, mid)
            return jnp.where(jnp.logical_and(lane >= COPY0 + 2, lane < COPY0 + 4), right, value)

        row_weights = {a: side_weights(a) for a in (-1, 0, 1)}

        def blend(i, l):
            at, row = i * 8, ROW0[l] + i * 8
            if not isinstance(i, int):
                at, row = pl.multiple_of(at, 8), pl.multiple_of(row, 8)
            mask = None
            for a in range(3):
                term = rowc[pl.ds(SPREAD_AT + 184 * a + row, 8), :][:, None, :] * inner[HALF[l]][a][None]
                mask = term if mask is None else mask + term
            whole = jnp.sum(mask, axis=1)
            inverse = jnp.where(whole > 0.0, 1.0 / jnp.where(whole > 0.0, whole, 1.0), 0.0)
            for c in range(C):
                part = d[l][pl.ds(at, 8), V * c : V * c + V, :]
                planes[c, pl.ds(row, 8), :] = jnp.sum(part * mask, axis=1) * inverse
                if l == 1:
                    part = copies_ref[pl.ds(at, 8), V * c : V * c + V, :]
                    ones_ref[c, pl.ds(at, 8), :] = jnp.sum(part * row_weights[0][None], axis=1)

        def blend_rest(i, carry, l):
            blend(i, l)
            return carry

        for l, blocks in ((1, (0, 8, 9)), (2, (0, 4, 5)), (3, (0, 2, 3)), (4, (0, 1, 2))):
            for i in blocks:
                blend(i, l)

        for w in range(2):
            corners = [jnp.zeros((8, LANES), F32) for _ in range(2)]
            for c in range(C):
                at = {l: ROW0[l] + (SIDE[l] + 3 if w else 0) for l in range(1, 5)}
                halves = [planes[c, at[l] : at[l] + 8] + planes[c, at[l + 1] : at[l + 1] + 8] for l in (1, 3)]
                one = copies_ref[at[1] : at[1] + 8, V * c : V * c + V, :]
                one = jnp.sum(one * row_weights[1 if w else -1][None], axis=1)
                v_send[w, c, 0] = halves[0] - keep(one, 0, COPY0)
                v_send[w, c, 1] = halves[1]
                for side in range(2):
                    for l in range(1, 5):
                        slot = 8 * (4 * c + l - 1)
                        first = LANE0[l] + (SIDE[l] + 3 if side else 0)
                        corners[side] += keep(turn(halves[HALF[l]], slot - first), slot, slot + 6)
                    slot, first = (32 * c, COPY0 + 2) if side else (32 * c + 3, COPY0)
                    corners[side] -= keep(turn(one, slot - first), slot, slot + 2)
            for side in range(2):
                c_send[2 * w + side] = corners[side]
        v_rims = post(v_recv, [(v_send.at[w], v_recv.at[w], (2 * w - 1, 0)) for w in range(2)])
        ends = [(i, 2 * (i // 2) - 1, 2 * (i % 2) - 1) for i in range(4)]
        c_rims = post(c_recv, [(c_send.at[i], c_recv.at[i], (a, b)) for i, a, b in ends])
        for l, first, last in ((1, 1, 8), (2, 1, 4), (3, 1, 2)):
            lax.fori_loop(first, last, lambda i, carry, l=l: blend_rest(i, carry, l), 0)
        for which in range(2):
            for g in range(SIDE_TILES):
                tile = jnp.zeros((8, LANES), F32)
                for u, (c, l, row) in enumerate(ITEMS[16 * g : 16 * g + 16]):
                    first = LANE0[l] + (SIDE[l] + 3 if which else 0)
                    tile = tile + keep(turn(planes[c, row : row + 8], 8 * u - first), 8 * u, 8 * u + 6)
                    if l == 1:
                        slot, first = (8 * u, COPY0 + 2) if which else (8 * u + 3, COPY0)
                        tile = tile - keep(turn(ones_ref[c, row : row + 8], slot - first), slot, slot + 2)
                h_send[which, g] = tile
        h_rims = post(h_recv, [(h_send.at[w], h_recv.at[w], (0, 2 * w - 1)) for w in range(2)])
        for c in range(C):
            planes[c, 0:80] -= keep(ones_ref[c], 0, COPY0)

        own_weights = weights(own_mask)
        for c in range(C):
            total = None
            for v in range(V):
                term = x_ref[(v * C + c) * BLOCK : (v * C + c + 1) * BLOCK, :] * own_weights[v : v + 1, :]
                total = term if total is None else total + term
            xs_ref[c] = total

        v_rims.wait_recv()
        c_rims.wait_recv()
        h_rims.wait_recv()
        for w, a in ((1, -1), (0, 1)):
            flag = inside(a, 0)
            for c in range(C):
                for l in range(1, 5):
                    at, low = ROW0[l] + (3 if a < 0 else SIDE[l]), LANE0[l]
                    got = v_recv[w, c, HALF[l]][0:6] * flag
                    planes[c, at : at + 6] += keep(got, low, low + SIDE[l] + 9)
            for side, b in ((1, -1), (0, 1)):
                got = c_recv[2 * w + side][0:6] * inside(a, b)
                for c in range(C):
                    for l in range(1, 5):
                        at, slot = ROW0[l] + (3 if a < 0 else SIDE[l]), 8 * (4 * c + l - 1)
                        first = LANE0[l] + (3 if b < 0 else SIDE[l])
                        planes[c, at : at + 6] += keep(turn(got, first - slot), first, first + 6)
        for which, b in ((1, -1), (0, 1)):
            flag = inside(0, b)
            for i, (c, l, row) in enumerate(ITEMS):
                u = i % 16
                first = LANE0[l] + (3 if b < 0 else SIDE[l])
                got = h_recv[which, i // 16] * flag
                planes[c, row : row + 8] += keep(turn(got, first - 8 * u), first, first + 6)

        def wide_dot(a, b):
            return jnp.dot(a, b, precision=lax.Precision.HIGH, preferred_element_type=F32)

        upper = wide_dot(jnp.concatenate([planes[c, 0:128] for c in range(C)], axis=0), cols[0:128])
        lower = wide_dot(jnp.concatenate([planes[c, 128:192] for c in range(C)], axis=0), cols[128:256])
        across = [jnp.concatenate([upper[128 * c : 128 * c + 128], lower[64 * c : 64 * c + 64]], axis=0) for c in range(C)]
        total = wide_dot(
            jnp.concatenate([rowc[0:128], rowc[128:256]], axis=1)[:, 0:192], jnp.concatenate(across, axis=1)
        )
        for c in range(C):
            xs_ref[c] += total[:, LANES * c : LANES * c + LANES]

        for group in t_cols:
            group.wait_recv()
        tops_all = gather_tops(t_send[1], t_col, tp_col, tl_col, "col")
        flat = [cols[FLAT_AT : FLAT_AT + LANES], cols[FLAT_AT + LANES : FLAT_AT + 2 * LANES]]
        images, mask = tops_all[0:24], tops_all[24:32]
        whole = jnp.sum(mask, axis=0, keepdims=True)
        here = whole > 0.0
        share = mask * jnp.where(here, 1.0 / jnp.where(here, whole, 1.0), 0.0)
        finer = jnp.dot(images, flat[0] + flat[1], precision=lax.Precision.HIGHEST, preferred_element_type=F32)
        detail = images - finer
        blended = [jnp.sum(detail[V * c : V * c + V] * share, axis=0, keepdims=True) for c in range(C)]
        balance = keep(jnp.sum(share, axis=0, keepdims=True) * (1.0 / V) - share, FLAT0[7], FLAT0[7] + 16)
        chain = jnp.concatenate(blended + [jnp.zeros((8 - C, LANES), F32), balance], axis=0)
        for which in range(2):
            step = jnp.dot(chain, flat[which], precision=lax.Precision.HIGHEST, preferred_element_type=F32)
            chain = chain + jnp.where(here, step, 0.0)

        diagonal = jnp.logical_and(lane // 7 == view, lane < 49)
        spread = [jnp.where(diagonal, jnp.broadcast_to(chain[u : u + 1], (8, LANES)), 0.0) for u in (*range(C), *range(8, 16))]
        wide = wide_dot(jnp.concatenate(spread, axis=0), cols[FLAT_AT + 256 : FLAT_AT + 384])
        each = [wide[8 * u : 8 * u + 8] for u in range(C + V)]
        total = wide_dot(rowc[128:256, 56:64], jnp.concatenate(each, axis=1))
        for c in range(C):
            xs_ref[c] += total[:, LANES * c : LANES * c + LANES]
        for v in range(V):
            w_ref[v] = total[:, LANES * (C + v) : LANES * (C + v) + LANES]

        m_rows.wait_recv()
        means = m_send[1] + jnp.sum(m_row[...], axis=0)
        each = [jnp.broadcast_to(means[:, i : i + 1], (8, LANES)) for i in range(V * C)]
        for i in range(BLOCK // 8):
            added = [w_ref[v, 8 * i : 8 * i + 8] for v in range(V)]
            for c in range(C):
                total = xs_ref[c, 8 * i : 8 * i + 8]
                for v in range(V):
                    total = total + each[V * c + v] * added[v]
                out_ref[c, 8 * i : 8 * i + 8] = total

        for group in groups:
            group.wait_send()

    def vmem(*shape):
        return pltpu.VMEM(shape, F32)

    slabs = [vmem(n, 24, LANES) for n in (80, 48, 32, 24, 16, 16, 16)]
    wides = [vmem(ROWS[l], 24, LANES) for l in range(1, 5)]
    scratch = [
        vmem(V * C * BLOCK, LANES),
        pltpu.VMEM((N_MATS, 2 * LANES), jnp.bfloat16),
        vmem(N_COLS, LANES),
        vmem(N_ROWC, LANES),
        *slabs, *wides, *wides,
        vmem(80, 24, LANES),
        vmem(C, BLOCK, LANES),
        vmem(C, 192, LANES),
        vmem(C, 80, LANES),
        vmem(2, 1, LANES),
        vmem(nc - 1, 1, LANES),
        vmem(nr - 1, 1, LANES),
        vmem(V, LANES),
        vmem(8, V, LANES),
        vmem(2, 32, LANES),
        vmem(2, 16, LANES),
        vmem(2, 8, LANES),
        *[vmem(2, n, LANES) for n in (32, 16, 8, 32, 16, 8)],
        vmem(2, C, 2, 8, LANES),
        vmem(2, C, 2, 8, LANES),
        vmem(2, SIDE_TILES, 8, LANES),
        vmem(2, SIDE_TILES, 8, LANES),
        vmem(4, 8, LANES),
        vmem(4, 8, LANES),
        vmem(V, BLOCK, LANES),
        pltpu.SemaphoreType.DMA((8,)),
        pltpu.SemaphoreType.DMA((12,)),
        pltpu.SemaphoreType.DMA((12,)),
        pltpu.SemaphoreType.REGULAR,
    ]
    return pl.pallas_call(
        kernel,
        out_shape=jax.ShapeDtypeStruct((C, BLOCK, BLOCK), F32),
        in_specs=[pl.BlockSpec(memory_space=pltpu.SMEM)] * 2 + [pl.BlockSpec(memory_space=pl.ANY)] * 4,
        out_specs=pl.BlockSpec(memory_space=pltpu.VMEM),
        scratch_shapes=scratch,
        compiler_params=pltpu.CompilerParams(collective_id=0, has_side_effects=True, vmem_limit_bytes=54500 << 10),
    )


def solution(mesh):
    call = make_kernel(mesh.shape["row"], mesh.shape["col"])

    def local(view_images, intersection_bits, seam_labels):
        planes = view_images.reshape(V * C * BLOCK, BLOCK)
        return call(
            intersection_bits, seam_labels, planes,
            jnp.asarray(MATS), jnp.asarray(COLS), jnp.asarray(ROWC),
        )

    placed = (P(None, None, "row", "col"), P("row", "col"), P("row", "col"))
    return jax.shard_map(local, mesh=mesh, in_specs=placed, out_specs=P(None, "row", "col"), check_vma=False)
```
